128 devices in a mesh: grp: 4 (over x), side: 2 (over core), seq: 16 (over y, z).
Axes of the slice: x: 4, y: 4, z: 4, core: 2. Of those that a mesh axis runs over, the one named last changes fastest.
Arguments:
- queries: bfloat16 [2, 4, 1024, 64, 576], P('side', 'grp', 'seq'), may hold values from -48 to 48
- stream_rows: bfloat16 [2, 4, 1024, 576], P('side', 'grp', 'seq'), may hold values from -6 to 6
- span_latents: bfloat16 [4, 1024, 576], P('grp', 'seq'), may hold values from -6 to 6
- decode_cache: bfloat16 [262144, 576], P(('grp', 'seq')), may hold values from -6 to 6
- cache_lengths: int32 [64, 64], P(('grp', 'seq')), may hold values from 1 to 256, 4096 in all within a row
- block_owner: int32 [128, 1], replicated, may hold values from 0 to 63; in each aligned block of 128 rows (0 to 127, 128 to 255, ...) at most 4 rows name the same one
- block_request: int32 [128], replicated, may hold values from 0 to 63
Outputs:
- attended: bfloat16 [2, 4, 1024, 64, 512], P('side', 'grp', 'seq')
The draws below stay inside these ranges and needn't reach their ends.
Inputs may be any that keep to these rules, and one draw needn't show every extreme that they name: Each row of cache_lengths sums to 4096; a device's requests take consecutive rows of its 4096 resident rows in order. `block_owner`: decode devices are numbered grp index * 16 + seq index; no device receives more than 4 blocks.
All inputs are finite; a program needn't handle non-finite values.
Results may differ from the reference program's by a relative error of at most 0.0048.
Values may be sent and summed in bfloat16 or wider, within the bound.
A program may use at most 128 MiB of HBM per device.

```python
import math
import jax
import jax.numpy as jnp
import numpy as np
from jax import lax

HEADS = 64
LAT = 512
ROPE = 64
NOPE = 128
QROWS = 64
BLOCK = 32
CTX = 64
WIDE = 576
SPAN = 1024
MAXIN = 4
POOL = 4096
MOSTLEN = 256
OWNERS = 64
BLOCKS = 128
N_GRP = 4
N_SEQ = 16


def draw_stream_rows(key, part):
    shape = (2, N_GRP, SPAN, LAT + ROPE)
    noise = jax.random.normal(jax.random.fold_in(key, 11), shape, jnp.float32)
    values = noise
    return jnp.clip(values, -6.0, 6.0).astype(jnp.bfloat16)


def draw_span_latents(key, part):
    shape = (N_GRP, SPAN, LAT + ROPE)
    noise = jax.random.normal(jax.random.fold_in(key, 12), shape, jnp.float32)
    values = noise
    return jnp.clip(values, -6.0, 6.0).astype(jnp.bfloat16)


def draw_decode_cache(key, part):
    shape = (N_GRP * N_SEQ * QROWS * CTX, LAT + ROPE)
    noise = jax.random.normal(jax.random.fold_in(key, 13), shape, jnp.float32)
    values = noise
    return jnp.clip(values, -6.0, 6.0).astype(jnp.bfloat16)


def draw_queries(key, part):
    shape = (2, N_GRP, SPAN, HEADS, LAT + ROPE)
    noise = jax.random.normal(jax.random.fold_in(key, 14), shape, jnp.float32)
    values = noise
    return jnp.clip(values, -48.0, 48.0).astype(jnp.bfloat16)


def with_ends(drawn, rng, least, high):
    spot = [jax.random.randint(jax.random.fold_in(rng, axis), (), 0, length) for axis, length in enumerate(drawn.shape)]
    longest = drawn.shape.index(max(drawn.shape))
    next_to = spot[:longest] + [(spot[longest] + 1) % drawn.shape[longest]] + spot[longest + 1:]
    return drawn.at[tuple(spot)].set(least).at[tuple(next_to)].set(high)


def length_profile(number_of, total, reach, lean):
    portions = [(1 << 20) // math.isqrt(grade ** lean) + 1 for grade in range(2, number_of + 1)]
    surplus, holding = total - reach - (number_of - 1), [1] * (number_of - 1)
    while surplus > 0:
        movable = [i for i in range(number_of - 1) if holding[i] < reach]
        pool, left = sum([portions[i] for i in movable]), surplus
        for i in movable:
            more = min(reach - holding[i], max(1, left * portions[i] // pool), surplus)
            holding[i] = holding[i] + more
            surplus = surplus - more
    return np.array([reach] + holding)


def ragged_sizes(own_key, number_of, total, limit, lean):
    if number_of == 2:
        one = jax.random.randint(own_key, (), max(1, total - limit), min(limit, total - 1) + 1)
        return jnp.stack([one, total - one])
    tallies = jnp.asarray(length_profile(number_of, total, limit, lean), jnp.int32)
    couples = (number_of - 1) // 2
    giver, sink = tallies[1:1 + 2 * couples:2], tallies[2:2 + 2 * couples:2]
    slack = jnp.minimum(giver - 1, limit - sink)
    moved = jax.random.randint(jax.random.fold_in(own_key, 1), (couples,), 0, 1 << 20) % (slack + 1)
    tallies = tallies.at[1:1 + 2 * couples:2].set(giver - moved).at[2:2 + 2 * couples:2].set(sink + moved)
    return tallies[jax.random.permutation(jax.random.fold_in(own_key, 2), number_of)]


def shared_out(stream_key, own, number, rows, amount, top, bound, lean):
    sequence = jax.random.permutation(stream_key, amount)
    crowded, usual = load_shares(amount, rows * top, bound, lean, True), load_shares(amount, rows * top, bound, lean, False)
    places = jnp.arange(amount)

    def named(tallies, turn):
        used = int((tallies > 0).sum())
        fixed = max(1, used // 4)
        passed = fixed + (places - fixed + turn * (used - fixed)) % max(1, amount - fixed)
        return jnp.zeros((amount,), jnp.int32).at[sequence[jnp.where(places < fixed, places, passed)]].set(jnp.asarray(tallies, jnp.int32))

    tallies = jnp.where(number % 4 == 0, named(crowded, number // 4), named(usual, number - number // 4 - 1))
    mixed = jax.random.permutation(jax.random.fold_in(own, 3), amount)
    donor, taker = mixed[0:amount // 2 * 2:2], mixed[1:amount // 2 * 2:2]
    room = jnp.minimum(tallies[donor] - 1, bound - tallies[taker]) // 2
    room = jnp.where((donor == sequence[0]) | (taker == sequence[0]) | (tallies[taker] == 0), 0, jnp.maximum(room, 0))
    passed = jax.random.randint(jax.random.fold_in(own, 4), (amount // 2,), 0, 1 << 20) % (room + 1)
    tallies = tallies.at[donor].add(-passed).at[taker].add(passed)
    items = jnp.searchsorted(jnp.cumsum(tallies), jnp.arange(rows * top), side="right").astype(jnp.int32)
    table = items.reshape(top, rows).T
    table = table[jax.random.permutation(jax.random.fold_in(own, 1), rows)]
    turn = jax.random.randint(jax.random.fold_in(own, 2), (rows, 1), 0, top)
    return jnp.take_along_axis(table, (jnp.arange(top)[None, :] + turn) % top, axis=1)


def load_shares(amount, total, reach, lean, full):
    portions = [(1 << 20) // math.isqrt(standing ** lean) + 1 for standing in range(1, amount + 1)]
    largest = reach if full else min(reach, max(-(-total // amount), total * portions[0] // sum(portions)))
    least = 1 if total - largest >= amount - 1 else 0
    given, rest = [largest] + [least] * (amount - 1), total - largest - least * (amount - 1)
    while rest > 0:
        free = [i for i in range(1, amount) if given[i] < largest] or [i for i in range(1, amount) if given[i] < reach]
        mass, budget = sum([portions[i] for i in free]), rest
        for i in free:
            addition = min(reach - given[i], max(1, budget * portions[i] // mass), rest)
            given[i] = given[i] + addition
            rest = rest - addition
    return np.array(given)


def setup_inputs(seed: int = 0) -> dict:
    key_list = jax.random.split(jax.random.key(seed), 8)
    queries = draw_queries(jax.random.fold_in(key_list[7], 71), 0)
    stream_rows = draw_stream_rows(jax.random.fold_in(key_list[7], 71), 0)
    span_latents = draw_span_latents(jax.random.fold_in(key_list[7], 71), 0)
    decode_cache = draw_decode_cache(jax.random.fold_in(key_list[7], 71), 0)
    cache_lengths = jax.vmap(lambda own: ragged_sizes(own, QROWS, POOL, MOSTLEN, 2))(jax.random.split(key_list[4], OWNERS)).reshape((OWNERS, QROWS)).astype(jnp.int32)
    block_owner_keys = jax.random.split(jax.random.fold_in(key_list[5], 1), BLOCKS // BLOCKS)
    block_owner_turns = jax.random.permutation(jax.random.fold_in(key_list[5], 3), BLOCKS // BLOCKS)
    block_owner = jax.vmap(lambda own, number: shared_out(jax.random.fold_in(key_list[5], 2), own, number, BLOCKS, OWNERS, 1, MAXIN, 2))(block_owner_keys, block_owner_turns).reshape((BLOCKS, 1))
    block_request = with_ends(jax.random.randint(key_list[6], (BLOCKS,), 0, QROWS), jax.random.fold_in(key_list[6], 1), 0, QROWS - 1).astype(jnp.int32)
    return {"queries": queries, "stream_rows": stream_rows, "span_latents": span_latents, "decode_cache": decode_cache, "cache_lengths": cache_lengths, "block_owner": block_owner, "block_request": block_request}


def masked_weights(score_rows, allowed):
    masked = jnp.where(allowed, score_rows, -jnp.inf)
    largest = lax.optimization_barrier(jnp.max(masked, axis=-1, keepdims=True))
    lifted = jnp.exp(masked - largest)
    return (lifted / lax.optimization_barrier(jnp.sum(lifted, axis=-1, keepdims=True))).astype(jnp.bfloat16)

def prefill_group(group_query, key_rows):
    factor = 1.0 / math.sqrt(NOPE + ROPE)
    allowed = (jnp.arange(2 * SPAN) - SPAN)[None, :] <= jnp.arange(SPAN)[:, None]
    key_wide = key_rows.astype(jnp.float32)

    def one_head(head_query):
        scored = jnp.einsum('qw,kw->qk', head_query.astype(jnp.float32), key_wide, precision=lax.Precision.HIGHEST) * factor
        weights = masked_weights(scored, allowed)
        return jnp.einsum('qk,kl->ql', weights.astype(jnp.float32), key_wide[:, :LAT], precision=lax.Precision.HIGHEST).astype(jnp.bfloat16)
    per_head = lax.map(one_head, jnp.transpose(group_query, (1, 0, 2)))
    return jnp.transpose(per_head, (1, 0, 2))

def reference(queries, stream_rows, span_latents, decode_cache, cache_lengths, block_owner, block_request):
    factor = 1.0 / math.sqrt(NOPE + ROPE)
    prefill = jnp.stack([prefill_group(queries[0, grp_number], jnp.concatenate([stream_rows[0, grp_number], span_latents[grp_number]], 0)) for grp_number in range(N_GRP)])
    owners = block_owner[:, 0]
    blocks_all = stream_rows[0].reshape(BLOCKS, BLOCK, WIDE)
    block_ids = jnp.arange(BLOCKS, dtype=jnp.int32)

    def one_owner(inputs):
        owner, owner_query, own_latent, pool_rows, lengths = inputs
        order_key = jnp.where(owners == owner, block_ids, BLOCKS + block_ids)
        picked = jnp.argsort(order_key)[:MAXIN]
        present = owners[picked] == owner
        requests = block_request[picked]
        arrived = blocks_all[picked].reshape(MAXIN * BLOCK, WIDE).astype(jnp.float32)
        arrived_allowed = jnp.repeat(present[None, :] & (requests[None, :] == jnp.arange(QROWS)[:, None]), BLOCK, axis=1)
        offsets = (jnp.cumsum(lengths) - lengths).astype(jnp.int32)
        padded = jnp.concatenate([pool_rows.astype(jnp.float32), jnp.zeros((MOSTLEN, WIDE), jnp.float32)], 0)
        windows = jax.vmap(lambda offset: lax.dynamic_slice_in_dim(padded, offset, MOSTLEN, 0))(offsets)
        query_wide = owner_query.astype(jnp.float32)
        latent_wide = own_latent.astype(jnp.float32)
        resident = jnp.einsum('rhw,rtw->rht', query_wide, windows, precision=lax.Precision.HIGHEST)
        incoming = jnp.einsum('rhw,kw->rhk', query_wide, arrived, precision=lax.Precision.HIGHEST)
        itself = jnp.einsum('rhw,rw->rh', query_wide, latent_wide, precision=lax.Precision.HIGHEST)[:, :, None]
        scored = jnp.concatenate([resident, incoming, itself], -1) * factor
        resident_allowed = jnp.arange(MOSTLEN)[None, :] < lengths[:, None]
        allowed = jnp.concatenate([resident_allowed, arrived_allowed, jnp.ones((QROWS, 1), jnp.bool_)], -1)[:, None, :]
        weights = masked_weights(scored, allowed).astype(jnp.float32)
        context = jnp.einsum('rht,rtl->rhl', weights[:, :, :MOSTLEN], windows[:, :, :LAT], precision=lax.Precision.HIGHEST)
        context = context + jnp.einsum('rhk,kl->rhl', weights[:, :, MOSTLEN:MOSTLEN + MAXIN * BLOCK], arrived[:, :LAT], precision=lax.Precision.HIGHEST)
        context = context + weights[:, :, MOSTLEN + MAXIN * BLOCK:] * latent_wide[:, None, :LAT]
        return context.astype(jnp.bfloat16)
    decoded = lax.map(one_owner, (jnp.arange(OWNERS, dtype=jnp.int32), queries[1].reshape(OWNERS, QROWS, HEADS, WIDE), stream_rows[1].reshape(OWNERS, QROWS, WIDE), decode_cache.reshape(OWNERS, POOL, WIDE), cache_lengths))
    return jnp.stack([prefill, decoded.reshape(N_GRP, SPAN, HEADS, LAT)])
```

```python
import functools
import math

import jax
import jax.numpy as jnp
from jax import lax
from jax.experimental import pallas as pl
from jax.experimental.pallas import tpu as pltpu
from jax.sharding import PartitionSpec as P

LAT = 512
WIDE = 576
HEADS = 64
ROWS = 64
VEC = ROWS * HEADS
SCALE = 1.4426950408889634 / math.sqrt(192.0)
LOW = -1e30
MESH = pl.DeviceIdType.MESH
F32 = jnp.float32
BF16 = jnp.bfloat16
UNIT = 256
NT = (((1,), (1,)), ((), ()))


def dot_nt(a, b):
    return lax.dot_general(a, b, NT, preferred_element_type=F32)


def dot_nn(a, b):
    return jnp.dot(a, b, preferred_element_type=F32)


PAIRS = 32


def decode_kernel(
    q_hbm, kt_hbm, lat_hbm, len_ref, out_hbm, tok_ref,
    qv, kt, lat, ov, selfs, s0, s1, p0, p1, m0, m1, l0, l1, mrun, lrun, acc,
    starts, pc, pt, qsem, ksem, lsem, osem,
):
    side = lax.axis_index("side")
    tok_ref[0, 0] = 0

    def q_copy(c):
        r = pl.ds(pl.multiple_of(c * 256, 256), 256)
        return pltpu.make_async_copy(q_hbm.at[r, :], qv.at[r, :], qsem.at[c])

    def k_copy(t):
        r = pl.ds(pl.multiple_of(t * 256, 256), 256)
        return pltpu.make_async_copy(kt_hbm.at[:, r], kt.at[:, r], ksem.at[t])

    def o_copy(c):
        r = pl.ds(pl.multiple_of(c * 256, 256), 256)
        return pltpu.make_async_copy(ov.at[r, :], out_hbm.at[r, :], osem.at[c])

    @pl.when(side == 1)
    def _():
        lat_copy = pltpu.make_async_copy(lat_hbm, lat, lsem)
        lat_copy.start()
        for c in range(16):
            q_copy(c).start()
        for t in range(16):
            k_copy(t).start()

        def scan(r, total):
            starts[r] = total
            return total + len_ref[0, r]

        starts[64] = lax.fori_loop(0, 64, scan, jnp.int32(0))

        def fill(p, carry):
            c, t = carry
            pc[p] = jnp.minimum(c, 15)
            pt[p] = jnp.where(c < 16, t, -1)
            cc = jnp.minimum(c, 15)
            end = starts[cc * 4 + 4]
            more = (t + 1) * UNIT < end
            nc = jnp.where(more, c, c + 1)
            ns = starts[jnp.minimum(nc, 15) * 4]
            nt = jnp.where(more, t + 1, ns // UNIT)
            return nc, nt

        lax.fori_loop(0, PAIRS, fill, (jnp.int32(0), jnp.int32(0)))
        lat_copy.wait()

        def own(c, _):
            q_copy(c).wait()
            for k in range(4):
                r = c * 4 + k
                row = jnp.sum(
                    jnp.where(
                        lax.broadcasted_iota(jnp.int32, (64, WIDE), 0) == r,
                        lat[...].astype(F32), 0.0,
                    ),
                    axis=0, keepdims=True,
                )
                rr = pl.ds(pl.multiple_of(r * 64, 64), 64)
                d = jnp.sum(qv[rr, :].astype(F32) * row, axis=1, keepdims=True)
                selfs[rr, :] = jnp.broadcast_to(d, (64, 128))
            return 0

        lax.fori_loop(0, 16, own, 0)
        for t in range(16):
            k_copy(t).wait()

        def cols(p):
            t = jnp.maximum(pt[p], 0)
            return pl.ds(pl.multiple_of(t * UNIT, UNIT), UNIT)

        def crows(p):
            return pl.ds(pl.multiple_of(pc[p] * 256, 256), 256)

        def qk(p, s):
            s[...] = dot_nn(qv[crows(p), :], kt[:, cols(p)])

        def soft(p, s, pr, m, l):
            c, t = pc[p], pt[p]
            base = t * UNIT
            for k in range(4):
                rr = slice(64 * k, 64 * k + 64)
                lo = jnp.where(t < 0, 1 << 20, starts[c * 4 + k] - base)
                hi = starts[c * 4 + k + 1] - base
                col = lax.broadcasted_iota(jnp.int32, (64, UNIT), 1)
                x = jnp.where((col >= lo) & (col < hi), s[rr, :], LOW)
                mx = jnp.max(x, axis=1, keepdims=True)
                e = jnp.exp2((x - mx) * SCALE)
                m[rr, :] = jnp.broadcast_to(mx, (64, 128))
                l[rr, :] = jnp.broadcast_to(jnp.sum(e, axis=1, keepdims=True), (64, 128))
                pr[rr, :] = e.astype(BF16)

        def pv(p, pr, m, l):
            c = pc[p]
            new = (p == 0) | (pc[jnp.maximum(p - 1, 0)] != c)
            o = dot_nt(pr[...], kt[:LAT, cols(p)])
            for k in range(4):
                rr = slice(64 * k, 64 * k + 64)
                r = c * 4 + k
                row = jnp.sum(
                    jnp.where(
                        lax.broadcasted_iota(jnp.int32, (64, LAT), 0) == r,
                        lat[:, :LAT].astype(F32), 0.0,
                    ),
                    axis=0, keepdims=True,
                )
                g = pl.ds(pl.multiple_of(r * 64, 64), 64)
                mo = jnp.where(new, selfs[g, :], mrun[rr, :])
                lo = jnp.where(new, 1.0, lrun[rr, :])
                ao = jnp.where(new, jnp.broadcast_to(row, (64, LAT)), acc[rr, :])
                mn = jnp.maximum(mo, m[rr, :])
                al = jnp.exp2((mo - mn) * SCALE)
                be = jnp.exp2((m[rr, :] - mn) * SCALE)
                ln = lo * al + l[rr, :] * be
                an = ao * al[:, :1] + o[rr, :] * be[:, :1]
                mrun[rr, :] = mn
                lrun[rr, :] = ln
                acc[rr, :] = an
                ov[g, :] = (an * (1.0 / ln[:, :1])).astype(BF16)

        qk(0, s0)
        qk(1, s1)
        soft(0, s0, p0, m0, l0)

        def body(i, done):
            j = 2 * i
            qk(j + 2, s0)
            soft(j + 1, s1, p1, m1, l1)
            pv(j, p0, m0, l0)
            qk(j + 3, s1)
            soft(j + 2, s0, p0, m0, l0)
            pv(j + 1, p1, m1, l1)
            now = pc[j + 2]

            def send(c, _):
                o_copy(c).start()
                return 0

            lax.fori_loop(done, now, send, 0)
            return now

        done = lax.fori_loop(0, PAIRS // 2 - 1, body, jnp.int32(0))
        soft(PAIRS - 1, s1, p1, m1, l1)
        pv(PAIRS - 2, p0, m0, l0)
        pv(PAIRS - 1, p1, m1, l1)

        def send(c, _):
            o_copy(c).start()
            return 0

        lax.fori_loop(done, 16, send, 0)
        for c in range(16):
            o_copy(c).wait()


def decode(q, kt, latent, lengths):
    any_ = pl.BlockSpec(memory_space=pl.ANY)
    smem = pl.BlockSpec(memory_space=pltpu.SMEM)
    v = pltpu.VMEM
    return pl.pallas_call(
        decode_kernel,
        out_shape=(
            jax.ShapeDtypeStruct((VEC, LAT), BF16),
            jax.ShapeDtypeStruct((8, 128), jnp.int32),
        ),
        in_specs=[any_, any_, any_, smem],
        out_specs=(any_, smem),
        scratch_shapes=[
            v((VEC, WIDE), BF16), v((WIDE, 4096), BF16), v((64, WIDE), BF16), v((VEC, LAT), BF16),
            v((VEC, 128), F32),
            v((256, UNIT), F32), v((256, UNIT), F32), v((256, UNIT), BF16), v((256, UNIT), BF16),
            v((256, 128), F32), v((256, 128), F32), v((256, 128), F32), v((256, 128), F32),
            v((256, 128), F32), v((256, 128), F32), v((256, LAT), F32),
            pltpu.SMEM((65,), jnp.int32), pltpu.SMEM((PAIRS,), jnp.int32), pltpu.SMEM((PAIRS,), jnp.int32),
            pltpu.SemaphoreType.DMA((16,)), pltpu.SemaphoreType.DMA((16,)),
            pltpu.SemaphoreType.DMA, pltpu.SemaphoreType.DMA((16,)),
        ],
        compiler_params=pltpu.CompilerParams(vmem_limit_bytes=56 << 20),
        name="decode_resident",
    )(q, kt, latent, lengths)


BQ = 256


def gather_kernel(
    stream_hbm, span_hbm, owner, tok, kv_hbm, blk_hbm,
    kv, sendb, recvb, insem, ssem, rsem, xssem, xrsem, osem, bsem, sib_ready, x_ready,
):
    g = lax.axis_index("grp")
    side = lax.axis_index("side")
    sq = lax.axis_index("seq")
    y, z = sq // 4, sq % 4
    yn, yp = (y + 1) % 4, (y + 3) % 4
    zn, zp = (z + 1) % 4, (z + 3) % 4
    barrier = pltpu.get_barrier_semaphore()
    zn_dev, zp_dev = y * 4 + zn, y * 4 + zp
    yn_dev, yp_dev = yn * 4 + z, yp * 4 + z

    def rows(start, size):
        return pl.ds(pl.multiple_of(start, 16), size)

    def remote(start, size, to, k):
        ref = kv.at[rows(start, size), :]
        return pltpu.make_async_remote_copy(
            src_ref=ref, dst_ref=ref, send_sem=ssem.at[k], recv_sem=rsem.at[k],
            device_id={"seq": to}, device_id_type=MESH,
        )

    def stream_at(yy, zz):
        return yy * 256 + zz * 64

    def span_at(yy, zz):
        return 1024 + zz * 256 + yy * 64

    def block_copy(to, k):
        return pltpu.make_async_remote_copy(
            src_ref=sendb.at[k], dst_ref=recvb.at[g], send_sem=xssem.at[k], recv_sem=xrsem.at[g],
            device_id={"grp": to, "side": 1}, device_id_type=MESH,
        )

    @pl.when(side == 0)
    def _():
        for to in (zn_dev, zp_dev, yn_dev, yp_dev):
            pl.semaphore_signal(barrier, inc=1, device_id={"seq": to}, device_id_type=MESH)
        for k in range(4):
            pl.semaphore_signal(
                barrier, inc=1, device_id={"grp": (g + k) % 4, "side": 1}, device_id_type=MESH
            )

    in_stream = pltpu.make_async_copy(stream_hbm, kv.at[rows(stream_at(y, z), 64), :], insem.at[0])
    in_span = pltpu.make_async_copy(span_hbm, kv.at[rows(span_at(y, z), 64), :], insem.at[1])

    @pl.when(side == 0)
    def _():
        in_stream.start()
        in_span.start()

    pl.semaphore_wait(barrier, 4)

    @pl.when(side == 1)
    def _():
        pl.semaphore_signal(sib_ready, inc=1, device_id={"side": 0}, device_id_type=MESH)
        for k in range(1, 4):
            pl.semaphore_signal(
                x_ready, inc=1, device_id={"grp": (g + k) % 4, "side": 0}, device_id_type=MESH
            )
        for k in range(4):
            pltpu.make_async_remote_copy(
                src_ref=sendb.at[k], dst_ref=recvb.at[k], send_sem=xssem.at[k], recv_sem=xrsem.at[k],
                device_id={"side": 0}, device_id_type=MESH,
            ).wait_recv()
        c = pltpu.make_async_copy(recvb, blk_hbm, bsem)
        c.start()
        c.wait()

    @pl.when(side == 0)
    def _():
        in_stream.wait()
        in_span.wait()
        r1 = [
            remote(stream_at(y, z), 64, zn_dev, 0),
            remote(stream_at(y, z), 64, zp_dev, 1),
            remote(span_at(y, z), 64, yn_dev, 2),
            remote(span_at(y, z), 64, yp_dev, 3),
        ]
        for c in r1:
            c.start()
        remote(stream_at(y, zp), 64, zn_dev, 0).wait_recv()
        remote(span_at(yp, z), 64, yn_dev, 2).wait_recv()
        remote(stream_at(y, zn), 64, zp_dev, 1).wait_recv()
        remote(span_at(yn, z), 64, yp_dev, 3).wait_recv()
        r2 = [
            remote(stream_at(y, zp), 32, zn_dev, 4),
            remote(stream_at(y, zn) + 32, 32, zp_dev, 5),
            remote(span_at(yp, z), 32, yn_dev, 6),
            remote(span_at(yn, z) + 32, 32, yp_dev, 7),
        ]
        for c in r2:
            c.start()
        zf, yf = (z + 2) % 4, (y + 2) % 4
        remote(stream_at(y, zf), 32, zn_dev, 4).wait_recv()
        remote(stream_at(y, zf) + 32, 32, zp_dev, 5).wait_recv()
        remote(span_at(yf, z), 32, yn_dev, 6).wait_recv()
        remote(span_at(yf, z) + 32, 32, yp_dev, 7).wait_recv()
        us, up = y * 256, 1024 + z * 256
        r3 = [
            remote(us, 256, yn_dev, 8),
            remote(us, 256, yp_dev, 9),
            remote(up, 256, zn_dev, 10),
            remote(up, 256, zp_dev, 11),
        ]
        for c in r3:
            c.start()

        usp, usn = yp * 256, yn * 256
        upp, upn = 1024 + zp * 256, 1024 + zn * 256
        remote(usp, 256, yn_dev, 8).wait_recv()
        remote(usn, 256, yp_dev, 9).wait_recv()
        remote(upp, 256, zn_dev, 10).wait_recv()
        remote(upn, 256, zp_dev, 11).wait_recv()
        r4 = [
            remote(usp, 128, yn_dev, 12),
            remote(usn + 128, 128, yp_dev, 13),
            remote(upp, 128, zn_dev, 14),
            remote(upn + 128, 128, zp_dev, 15),
        ]
        for c in r4:
            c.start()
        usf, upf = yf * 256, 1024 + zf * 256
        remote(usf, 128, yn_dev, 12).wait_recv()
        remote(usf + 128, 128, yp_dev, 13).wait_recv()
        remote(upf, 128, zn_dev, 14).wait_recv()
        remote(upf + 128, 128, zp_dev, 15).wait_recv()

        lane = lax.broadcasted_iota(jnp.int32, (1, 1024), 1)
        who = [((g + k) % 4) * 16 + sq for k in range(4)]

        def find(b, carry):
            o = owner[g * 32 + b]
            out = []
            for k in range(4):
                n, slots = carry[2 * k], carry[2 * k + 1]
                hit = jnp.where(o == who[k], 1, 0)
                slots = jnp.where(lane // 32 == b, n - (1 - hit) * 8, slots)
                out += [n + hit, slots]
            return tuple(out)

        found = lax.fori_loop(0, 32, find, (jnp.int32(0), jnp.full((1, 1024), -8, jnp.int32)) * 4)
        rowi = lax.broadcasted_iota(jnp.int32, (128, 1024), 0)
        coli = lax.broadcasted_iota(jnp.int32, (128, 1024), 1)
        same = rowi % 32 == coli % 32
        for k in range(4):
            pick = jnp.where(same & (found[2 * k + 1] == rowi // 32), 1.0, 0.0).astype(BF16)
            sendb[k] = dot_nn(pick, kv[:1024, :]).astype(BF16)
        pl.semaphore_wait(sib_ready, 1)
        pl.semaphore_wait(x_ready, 3)
        xb = [block_copy((g + k) % 4, k) for k in range(4)]
        for c in xb:
            c.start()

        outs = [
            pltpu.make_async_copy(kv.at[rows(u * UNIT, UNIT), :], kv_hbm.at[rows(u * UNIT, UNIT), :], osem.at[u])
            for u in range(8)
        ]
        for c in outs:
            c.start()
        for c in outs:
            c.wait()
        for c in r1 + r2 + r3 + r4 + xb:
            c.wait_send()


def gather(stream, span, owner, tok):
    any_ = pl.BlockSpec(memory_space=pl.ANY)
    smem = pl.BlockSpec(memory_space=pltpu.SMEM)
    v = pltpu.VMEM
    dma = pltpu.SemaphoreType.DMA
    return pl.pallas_call(
        gather_kernel,
        out_shape=(
            jax.ShapeDtypeStruct((2048, WIDE), BF16),
            jax.ShapeDtypeStruct((4, 128, WIDE), BF16),
        ),
        in_specs=[any_, any_, smem, any_],
        out_specs=(any_, any_),
        scratch_shapes=[
            v((2048, WIDE), BF16), v((4, 128, WIDE), BF16), v((4, 128, WIDE), BF16),
            dma((2,)), dma((16,)), dma((16,)), dma((4,)), dma((4,)), dma((8,)), dma,
            pltpu.SemaphoreType.REGULAR, pltpu.SemaphoreType.REGULAR,
        ],
        compiler_params=pltpu.CompilerParams(
            vmem_limit_bytes=32 << 20, collective_id=0, has_side_effects=True
        ),
        name="gather_latents",
    )(stream, span, owner, tok)


WIN = 384


def finish_kernel(
    q_hbm, kt_hbm, lat_hbm, len_ref, owner, request, kv_hbm, blk_hbm, old_hbm, out_hbm,
    qv, kv, sc, mx, p0, p1, l0, l1, o0, o1, pqsem, pksem, posem,
    lat, arr, qb, wb, ob, req, src, st, lsem, asem, qsem, wsem, osem,
):
    side = lax.axis_index("side")
    me = lax.axis_index("grp") * 16 + lax.axis_index("seq")

    @pl.when(side == 0)
    def _():
        sq = lax.axis_index("seq")

        def rows(start, size):
            return pl.ds(pl.multiple_of(start, 16), size)

        def q_copy(c):
            r = rows(c * 512, 512)
            return pltpu.make_async_copy(q_hbm.at[r, :], qv.at[r, :], pqsem.at[c])

        def k_copy(u):
            r = rows(u * UNIT, UNIT)
            return pltpu.make_async_copy(kv_hbm.at[r, :], kv.at[r, :], pksem.at[u])

        k_copy(0).start()
        for c in range(VEC // 512):
            q_copy(c).start()
        for u in range(1, 8):
            k_copy(u).start()

        def scores(unit, first, masked):
            keys = kv[rows(unit * UNIT, UNIT), :]
            cols = pl.ds(pl.multiple_of(unit * UNIT, UNIT), UNIT)

            def step(i, _):
                if first:
                    q_copy(i).wait()
                r = rows(i * 512, 512)
                x = dot_nt(qv[r, :], keys)
                if masked:
                    row = sq * 64 + i * 8 + lax.broadcasted_iota(jnp.int32, (512, UNIT), 0) // 64
                    j = lax.broadcasted_iota(jnp.int32, (512, UNIT), 1)
                    pos = ((j // 64) * 4 + (unit - 4)) * 64 + j % 64
                    x = jnp.where(pos <= row, x, LOW)
                sc[r, cols] = x
                top = jnp.maximum(x[:, :128], x[:, 128:])
                mx[r, :] = top if first else jnp.maximum(mx[r, :], top)
                return 0

            lax.fori_loop(0, VEC // 512, step, 0, unroll=2)

        for u in range(8):
            k_copy(u).wait()
            scores(u, u == 0, u >= 4)

        def soft(i, pr, l):
            r = rows(i * BQ, BQ)
            m = jnp.max(mx[r, :], axis=1, keepdims=True) * SCALE
            e = jnp.exp2(sc[r, :] * SCALE - m)
            pr[...] = e.astype(BF16)
            l[...] = jnp.broadcast_to(jnp.sum(e, axis=1, keepdims=True), (BQ, 128))

        def out_copy(i, o, b):
            return pltpu.make_async_copy(o, out_hbm.at[rows(i * BQ, BQ), :], posem.at[b])

        def values(i, pr, l, o):
            a = dot_nn(pr[...], kv[:, :LAT])
            o[...] = (a * (1.0 / l[:, :1])).astype(BF16)

        nb = VEC // BQ
        soft(0, p0, l0)

        def body(t, _):
            i = 2 * t

            @pl.when(t > 0)
            def _():
                out_copy(i - 2, o0, 0).wait()
                out_copy(i - 1, o1, 1).wait()

            soft(i + 1, p1, l1)
            values(i, p0, l0, o0)
            out_copy(i, o0, 0).start()
            soft((i + 2) % nb, p0, l0)
            values(i + 1, p1, l1, o1)
            out_copy(i + 1, o1, 1).start()
            return 0

        lax.fori_loop(0, nb // 2, body, 0)
        out_copy(nb - 2, o0, 0).wait()
        out_copy(nb - 1, o1, 1).wait()

    @pl.when(side == 1)
    def _():
        lc = pltpu.make_async_copy(lat_hbm, lat, lsem)
        lc.start()
        for i in range(4):
            req[i] = 0
            src[i] = 0

        def find(b, carry):
            n, rank = carry
            rank = jnp.where(b % 32 == 0, 0, rank)
            hit = owner[b] == me

            @pl.when(hit)
            def _():
                req[n] = request[b]
                src[n] = (b // 32) * 4 + rank

            h = hit.astype(jnp.int32)
            return n + h, rank + h

        n, _ = lax.fori_loop(0, 128, find, (jnp.int32(0), jnp.int32(0)))

        def scan(r, total):
            st[r] = total
            return total + len_ref[0, r]

        lax.fori_loop(0, 64, scan, jnp.int32(0))

        def fetch(i):
            r = req[i]
            s = src[i]
            w = jnp.minimum(st[r] // 128, (4096 - WIN) // 128) * 128
            a = pltpu.make_async_copy(
                blk_hbm.at[s // 4, pl.ds(pl.multiple_of((s % 4) * 32, 32), 32), :],
                arr.at[pl.ds(32 * i, 32), :], asem.at[i],
            )
            b = pltpu.make_async_copy(
                q_hbm.at[pl.ds(pl.multiple_of(r * 64, 64), 64), :], qb.at[i], qsem.at[i]
            )
            c = pltpu.make_async_copy(
                kt_hbm.at[:, pl.ds(pl.multiple_of(w, 128), WIN)], wb.at[i], wsem.at[i]
            )
            return w, (a, b, c)

        got = [fetch(i) for i in range(4)]
        for _, cs in got:
            for c in cs:
                c.start()
        lc.wait()
        for _, cs in got:
            for c in cs:
                c.wait()

        def out_copy(i):
            return pltpu.make_async_copy(
                ob.at[i], out_hbm.at[pl.ds(pl.multiple_of(req[i] * 64, 64), 64), :], osem.at[i]
            )

        writes = []
        for i in range(4):
            r = req[i]
            w = got[i][0]
            ok = i < n
            for j in range(i):
                ok = ok & (req[j] != r)
            writes.append(ok)

            @pl.when(ok)
            def _(i=i, r=r, w=w):
                q = qb[i]
                row = jnp.sum(
                    jnp.where(
                        lax.broadcasted_iota(jnp.int32, (64, WIDE), 0) == r, lat[...].astype(F32), 0.0
                    ),
                    axis=0, keepdims=True,
                )
                x3 = jnp.sum(q.astype(F32) * row, axis=1, keepdims=True)
                x1 = dot_nn(q, wb[i])
                col = lax.broadcasted_iota(jnp.int32, (64, WIN), 1) + w
                x1 = jnp.where((col >= st[r]) & (col < st[r] + len_ref[0, r]), x1, LOW)
                x2 = dot_nt(q, arr[...])
                slot = lax.broadcasted_iota(jnp.int32, (64, 128), 1) // 32
                seen = (slot == 0) & (0 < n) & (req[0] == r)
                for j in range(1, 4):
                    seen = seen | ((slot == j) & ((j < n) & (req[j] == r)))
                x2 = jnp.where(seen, x2, LOW)
                m = jnp.maximum(
                    x3,
                    jnp.maximum(
                        jnp.max(x1, axis=1, keepdims=True), jnp.max(x2, axis=1, keepdims=True)
                    ),
                )
                e1 = jnp.exp2((x1 - m) * SCALE)
                e2 = jnp.exp2((x2 - m) * SCALE)
                e3 = jnp.exp2((x3 - m) * SCALE)
                l = jnp.sum(e1, axis=1, keepdims=True) + jnp.sum(e2, axis=1, keepdims=True) + e3
                o = dot_nt(e1.astype(BF16), wb[i, :LAT, :]) + dot_nn(e2.astype(BF16), arr[:, :LAT])
                o = o + e3.astype(BF16).astype(F32) * row[:, :LAT]
                ob[i] = (o * (1.0 / l)).astype(BF16)
                out_copy(i).start()

        for i in range(4):
            @pl.when(writes[i])
            def _(i=i):
                out_copy(i).wait()


def finish(q, kt, latent, lengths, owner, request, kv, blocks, old):
    any_ = pl.BlockSpec(memory_space=pl.ANY)
    smem = pl.BlockSpec(memory_space=pltpu.SMEM)
    v = pltpu.VMEM
    dma = pltpu.SemaphoreType.DMA
    return pl.pallas_call(
        finish_kernel,
        out_shape=jax.ShapeDtypeStruct((VEC, LAT), BF16),
        in_specs=[any_, any_, any_, smem, smem, smem, any_, any_, any_],
        out_specs=any_,
        scratch_shapes=[
            v((VEC, WIDE), BF16), v((2048, WIDE), BF16), v((VEC, 2048), F32), v((VEC, 128), F32),
            v((BQ, 2048), BF16), v((BQ, 2048), BF16), v((BQ, 128), F32), v((BQ, 128), F32),
            v((BQ, LAT), BF16), v((BQ, LAT), BF16), dma((VEC // 512,)), dma((8,)), dma((2,)),
            v((64, WIDE), BF16), v((128, WIDE), BF16), v((4, 64, WIDE), BF16), v((4, WIDE, WIN), BF16),
            v((4, 64, LAT), BF16),
            pltpu.SMEM((4,), jnp.int32), pltpu.SMEM((4,), jnp.int32), pltpu.SMEM((64,), jnp.int32),
            dma, dma((4,)), dma((4,)), dma((4,)), dma((4,)),
        ],
        input_output_aliases={8: 0},
        compiler_params=pltpu.CompilerParams(vmem_limit_bytes=60 << 20),
        name="finish",
    )(q, kt, latent, lengths, owner, request, kv, blocks, old)


def local(queries, stream_rows, span_latents, decode_cache, cache_lengths, block_owner, block_request):
    q = queries.reshape(VEC, WIDE)
    stream = stream_rows.reshape(ROWS, WIDE)
    span = span_latents.reshape(ROWS, WIDE)
    kt = decode_cache.T
    owner = block_owner.reshape(128)
    resident, tok = decode(q, kt, stream, cache_lengths)
    kv, blocks = gather(stream, span, owner, tok)
    out = finish(q, kt, stream, cache_lengths, owner, block_request, kv, blocks, resident)
    return out.reshape(1, 1, ROWS, HEADS, LAT)


def solution(mesh):
    return jax.shard_map(
        local,
        mesh=mesh,
        in_specs=(
            P("side", "grp", "seq", None, None),
            P("side", "grp", "seq", None),
            P("grp", "seq", None),
            P(("grp", "seq"), None),
            P(("grp", "seq"), None),
            P(),
            P(),
        ),
        out_specs=P("side", "grp", "seq", None, None),
        check_vma=False,
    )
```

```python
import functools
import math

import jax
import jax.numpy as jnp
from jax import lax
from jax.experimental import pallas as pl
from jax.experimental.pallas import tpu as pltpu
from jax.sharding import PartitionSpec as P

LAT = 512
WIDE = 576
HEADS = 64
ROWS = 64
VEC = ROWS * HEADS
SCALE = 1.4426950408889634 / math.sqrt(192.0)
LOW = -1e30
MESH = pl.DeviceIdType.MESH
F32 = jnp.float32
BF16 = jnp.bfloat16
UNIT = 256
NT = (((1,), (1,)), ((), ()))


def dot_nt(a, b):
    return lax.dot_general(a, b, NT, preferred_element_type=F32)


def dot_nn(a, b):
    return jnp.dot(a, b, preferred_element_type=F32)


def gather_kernel(
    stream_hbm, span_hbm, owner, kv_hbm, blk_hbm,
    kv, sendb, recvb, insem, ssem, rsem, xssem, xrsem, osem, bsem, sib_ready, x_ready,
):
    g = lax.axis_index("grp")
    side = lax.axis_index("side")
    sq = lax.axis_index("seq")
    y, z = sq // 4, sq % 4
    yn, yp = (y + 1) % 4, (y + 3) % 4
    zn, zp = (z + 1) % 4, (z + 3) % 4
    barrier = pltpu.get_barrier_semaphore()
    zn_dev, zp_dev = y * 4 + zn, y * 4 + zp
    yn_dev, yp_dev = yn * 4 + z, yp * 4 + z

    def rows(start, size):
        return pl.ds(pl.multiple_of(start, 16), size)

    def remote(start, size, to, k):
        ref = kv.at[rows(start, size), :]
        return pltpu.make_async_remote_copy(
            src_ref=ref, dst_ref=ref, send_sem=ssem.at[k], recv_sem=rsem.at[k],
            device_id={"seq": to}, device_id_type=MESH,
        )

    def stream_at(yy, zz):
        return yy * 256 + zz * 64

    def span_at(yy, zz):
        return 1024 + zz * 256 + yy * 64

    def block_copy(to, k):
        return pltpu.make_async_remote_copy(
            src_ref=sendb.at[k], dst_ref=recvb.at[g], send_sem=xssem.at[k], recv_sem=xrsem.at[g],
            device_id={"grp": to, "side": 1}, device_id_type=MESH,
        )

    @pl.when(side == 0)
    def _():
        for to in (zn_dev, zp_dev, yn_dev, yp_dev):
            pl.semaphore_signal(barrier, inc=1, device_id={"seq": to}, device_id_type=MESH)
        for k in range(4):
            pl.semaphore_signal(
                barrier, inc=1, device_id={"grp": (g + k) % 4, "side": 1}, device_id_type=MESH
            )

    in_stream = pltpu.make_async_copy(stream_hbm, kv.at[rows(stream_at(y, z), 64), :], insem.at[0])
    in_span = pltpu.make_async_copy(span_hbm, kv.at[rows(span_at(y, z), 64), :], insem.at[1])

    @pl.when(side == 0)
    def _():
        in_stream.start()
        in_span.start()

    pl.semaphore_wait(barrier, 4)

    @pl.when(side == 1)
    def _():
        pl.semaphore_signal(sib_ready, inc=1, device_id={"side": 0}, device_id_type=MESH)
        for k in range(1, 4):
            pl.semaphore_signal(
                x_ready, inc=1, device_id={"grp": (g + k) % 4, "side": 0}, device_id_type=MESH
            )
        for k in range(4):
            pltpu.make_async_remote_copy(
                src_ref=sendb.at[k], dst_ref=recvb.at[k], send_sem=xssem.at[k], recv_sem=xrsem.at[k],
                device_id={"side": 0}, device_id_type=MESH,
            ).wait_recv()
        c = pltpu.make_async_copy(recvb, blk_hbm, bsem)
        c.start()
        c.wait()

    @pl.when(side == 0)
    def _():
        in_stream.wait()
        in_span.wait()
        r1 = [
            remote(stream_at(y, z), 64, zn_dev, 0),
            remote(stream_at(y, z), 64, zp_dev, 1),
            remote(span_at(y, z), 64, yn_dev, 2),
            remote(span_at(y, z), 64, yp_dev, 3),
        ]
        for c in r1:
            c.start()
        remote(stream_at(y, zp), 64, zn_dev, 0).wait_recv()
        remote(span_at(yp, z), 64, yn_dev, 2).wait_recv()
        remote(stream_at(y, zn), 64, zp_dev, 1).wait_recv()
        remote(span_at(yn, z), 64, yp_dev, 3).wait_recv()
        r2 = [
            remote(stream_at(y, zp), 32, zn_dev, 4),
            remote(stream_at(y, zn) + 32, 32, zp_dev, 5),
            remote(span_at(yp, z), 32, yn_dev, 6),
            remote(span_at(yn, z) + 32, 32, yp_dev, 7),
        ]
        for c in r2:
            c.start()
        zf, yf = (z + 2) % 4, (y + 2) % 4
        remote(stream_at(y, zf), 32, zn_dev, 4).wait_recv()
        remote(stream_at(y, zf) + 32, 32, zp_dev, 5).wait_recv()
        remote(span_at(yf, z), 32, yn_dev, 6).wait_recv()
        remote(span_at(yf, z) + 32, 32, yp_dev, 7).wait_recv()
        us, up = y * 256, 1024 + z * 256
        r3 = [
            remote(us, 256, yn_dev, 8),
            remote(us, 256, yp_dev, 9),
            remote(up, 256, zn_dev, 10),
            remote(up, 256, zp_dev, 11),
        ]
        for c in r3:
            c.start()

        usp, usn = yp * 256, yn * 256
        upp, upn = 1024 + zp * 256, 1024 + zn * 256
        remote(usp, 256, yn_dev, 8).wait_recv()
        remote(usn, 256, yp_dev, 9).wait_recv()
        remote(upp, 256, zn_dev, 10).wait_recv()
        remote(upn, 256, zp_dev, 11).wait_recv()
        r4 = [
            remote(usp, 128, yn_dev, 12),
            remote(usn + 128, 128, yp_dev, 13),
            remote(upp, 128, zn_dev, 14),
            remote(upn + 128, 128, zp_dev, 15),
        ]
        for c in r4:
            c.start()
        usf, upf = yf * 256, 1024 + zf * 256
        remote(usf, 128, yn_dev, 12).wait_recv()
        remote(usf + 128, 128, yp_dev, 13).wait_recv()
        remote(upf, 128, zn_dev, 14).wait_recv()
        remote(upf + 128, 128, zp_dev, 15).wait_recv()

        lane = lax.broadcasted_iota(jnp.int32, (1, 1024), 1)
        who = [((g + k) % 4) * 16 + sq for k in range(4)]

        def find(b, carry):
            o = owner[g * 32 + b]
            out = []
            for k in range(4):
                n, slots = carry[2 * k], carry[2 * k + 1]
                hit = jnp.where(o == who[k], 1, 0)
                slots = jnp.where(lane // 32 == b, n - (1 - hit) * 8, slots)
                out += [n + hit, slots]
            return tuple(out)

        found = lax.fori_loop(0, 32, find, (jnp.int32(0), jnp.full((1, 1024), -8, jnp.int32)) * 4)
        rowi = lax.broadcasted_iota(jnp.int32, (128, 1024), 0)
        coli = lax.broadcasted_iota(jnp.int32, (128, 1024), 1)
        same = rowi % 32 == coli % 32
        for k in range(4):
            pick = jnp.where(same & (found[2 * k + 1] == rowi // 32), 1.0, 0.0).astype(BF16)
            sendb[k] = dot_nn(pick, kv[:1024, :]).astype(BF16)
        pl.semaphore_wait(sib_ready, 1)
        pl.semaphore_wait(x_ready, 3)
        xb = [block_copy((g + k) % 4, k) for k in range(4)]
        for c in xb:
            c.start()

        outs = [
            pltpu.make_async_copy(kv.at[rows(u * UNIT, UNIT), :], kv_hbm.at[rows(u * UNIT, UNIT), :], osem.at[u])
            for u in range(8)
        ]
        for c in outs:
            c.start()
        for c in outs:
            c.wait()
        for c in r1 + r2 + r3 + r4 + xb:
            c.wait_send()


def gather(stream, span, owner):
    any_ = pl.BlockSpec(memory_space=pl.ANY)
    smem = pl.BlockSpec(memory_space=pltpu.SMEM)
    v = pltpu.VMEM
    dma = pltpu.SemaphoreType.DMA
    return pl.pallas_call(
        gather_kernel,
        out_shape=(
            jax.ShapeDtypeStruct((2048, WIDE), BF16),
            jax.ShapeDtypeStruct((4, 128, WIDE), BF16),
        ),
        in_specs=[any_, any_, smem],
        out_specs=(any_, any_),
        scratch_shapes=[
            v((2048, WIDE), BF16), v((4, 128, WIDE), BF16), v((4, 128, WIDE), BF16),
            dma((2,)), dma((16,)), dma((16,)), dma((4,)), dma((4,)), dma((8,)), dma,
            pltpu.SemaphoreType.REGULAR, pltpu.SemaphoreType.REGULAR,
        ],
        compiler_params=pltpu.CompilerParams(
            vmem_limit_bytes=32 << 20, collective_id=0, has_side_effects=True
        ),
        name="gather_latents",
    )(stream, span, owner)


PAIRS = 32
BQ = 256
WIN = 384


def rows(start, size):
    return pl.ds(pl.multiple_of(start, 16), size)


def prefill_side(q_hbm, kv_hbm, out_hbm, qv, kv, bias, s0, s1, p0, p1, l0, l1, o0, o1, qsem, ksem, osem):
    sq = lax.axis_index("seq")
    nb = VEC // BQ

    def q_copy(i):
        r = rows(i * BQ, BQ)
        return pltpu.make_async_copy(q_hbm.at[r, :], qv.at[r, :], qsem.at[i])

    def k_copy(u):
        r = rows(u * 512, 512)
        return pltpu.make_async_copy(kv_hbm.at[r, :], kv.at[r, :], ksem.at[u])

    q_copy(0).start()
    for u in range(4):
        k_copy(u).start()
    for i in range(1, nb):
        q_copy(i).start()
    row = sq * 64 + lax.broadcasted_iota(jnp.int32, (64, 1024), 0)
    j = lax.broadcasted_iota(jnp.int32, (64, 1024), 1)
    pos = (((j // 64) % 4) * 4 + j // 256) * 64 + j % 64
    bias[...] = jnp.where(pos <= row, 0.0, LOW)

    def scores(i, s):
        q_copy(i).wait()
        s[...] = dot_nt(qv[rows(i * BQ, BQ), :], kv[...])

    def soft(i, s, pr, l):
        for k in range(4):
            r = slice(64 * k, 64 * k + 64)
            xa = s[r, :1024]
            xb = s[r, 1024:] + bias[pl.ds(i * 4 + k, 1), :]
            m = jnp.maximum(
                jnp.max(xa, axis=1, keepdims=True), jnp.max(xb, axis=1, keepdims=True)
            ) * SCALE
            ea = jnp.exp2(xa * SCALE - m)
            eb = jnp.exp2(xb * SCALE - m)
            pr[r, :1024] = ea.astype(BF16)
            pr[r, 1024:] = eb.astype(BF16)
            t = jnp.sum(ea, axis=1, keepdims=True) + jnp.sum(eb, axis=1, keepdims=True)
            l[r, :] = jnp.broadcast_to(t, (64, 128))

    def out_copy(i, o, b):
        return pltpu.make_async_copy(o, out_hbm.at[rows(i * BQ, BQ), :], osem.at[b])

    def values(i, pr, l, o):
        a = dot_nn(pr[...], kv[:, :LAT])
        o[...] = (a * (1.0 / l[:, :1])).astype(BF16)

    for u in range(4):
        k_copy(u).wait()
    scores(0, s0)
    scores(1, s1)
    soft(0, s0, p0, l0)

    def body(t, _):
        i = 2 * t

        @pl.when(t > 0)
        def _():
            out_copy(i - 2, o0, 0).wait()
            out_copy(i - 1, o1, 1).wait()

        q_copy(i + 2).wait()
        q_copy(i + 3).wait()
        s0[...] = dot_nt(qv[rows((i + 2) * BQ, BQ), :], kv[...])
        soft(i + 1, s1, p1, l1)
        values(i, p0, l0, o0)
        out_copy(i, o0, 0).start()
        s1[...] = dot_nt(qv[rows((i + 3) * BQ, BQ), :], kv[...])
        soft(i + 2, s0, p0, l0)
        values(i + 1, p1, l1, o1)
        out_copy(i + 1, o1, 1).start()
        return 0

    lax.fori_loop(0, nb // 2 - 1, body, 0)
    out_copy(nb - 4, o0, 0).wait()
    out_copy(nb - 3, o1, 1).wait()
    soft(nb - 1, s1, p1, l1)
    values(nb - 2, p0, l0, o0)
    out_copy(nb - 2, o0, 0).start()
    values(nb - 1, p1, l1, o1)
    out_copy(nb - 1, o1, 1).start()
    out_copy(nb - 2, o0, 0).wait()
    out_copy(nb - 1, o1, 1).wait()


def decode_side(
    q_hbm, kt_hbm, lat_hbm, blk_hbm, len_ref, owner, request, out_hbm,
    qv, kt, lat, latf, ov, selfs, s0, s1, p0, p1, m0, m1, l0, l1, mrun, lrun, acc, arr, ob,
    starts, pc, pt, req, src, qsem, ksem, lsem, asem, osem, fsem,
):
    me = lax.axis_index("grp") * 16 + lax.axis_index("seq")

    def q_copy(c):
        r = rows(c * 256, 256)
        return pltpu.make_async_copy(q_hbm.at[r, :], qv.at[r, :], qsem.at[c])

    def k_copy(t):
        r = pl.ds(pl.multiple_of(t * 256, 256), 256)
        return pltpu.make_async_copy(kt_hbm.at[:, r], kt.at[:, r], ksem.at[t])

    def o_copy(c):
        r = rows(c * 256, 256)
        return pltpu.make_async_copy(ov.at[r, :], out_hbm.at[r, :], osem.at[c])

    lat_copy = pltpu.make_async_copy(lat_hbm, lat, lsem)
    lat_copy.start()
    for c in range(16):
        q_copy(c).start()
    for t in range(16):
        k_copy(t).start()

    def scan(r, total):
        starts[r] = total
        return total + len_ref[0, r]

    starts[64] = lax.fori_loop(0, 64, scan, jnp.int32(0))

    def fill(p, carry):
        c, t = carry
        pc[p] = jnp.minimum(c, 15)
        pt[p] = jnp.where(c < 16, t, -1)
        cc = jnp.minimum(c, 15)
        more = (t + 1) * UNIT < starts[cc * 4 + 4]
        nc = jnp.where(more, c, c + 1)
        ns = starts[jnp.minimum(nc, 15) * 4]
        nt = jnp.where(more, t + 1, ns // UNIT)
        return nc, nt

    lax.fori_loop(0, PAIRS, fill, (jnp.int32(0), jnp.int32(0)))
    for i in range(4):
        req[i] = 0
        src[i] = 0

    def find(b, carry):
        n, rank = carry
        rank = jnp.where(b % 32 == 0, 0, rank)
        hit = owner[b] == me

        @pl.when(hit)
        def _():
            req[n] = request[b]
            src[n] = (b // 32) * 4 + rank

        h = hit.astype(jnp.int32)
        return n + h, rank + h

    n, _ = lax.fori_loop(0, 128, find, (jnp.int32(0), jnp.int32(0)))
    arrivals = []
    for i in range(4):
        s = src[i]
        arrivals.append(
            pltpu.make_async_copy(
                blk_hbm.at[s // 4, pl.ds(pl.multiple_of((s % 4) * 32, 32), 32), :],
                arr.at[pl.ds(32 * i, 32), :], asem.at[i],
            )
        )
    for c in arrivals:
        c.start()
    lat_copy.wait()
    latf[...] = lat[...].astype(F32)

    def own(c, _):
        q_copy(c).wait()
        for k in range(4):
            r = c * 4 + k
            rr = pl.ds(pl.multiple_of(r * 64, 64), 64)
            d = jnp.sum(qv[rr, :].astype(F32) * latf[pl.ds(r, 1), :], axis=1, keepdims=True)
            selfs[rr, :] = jnp.broadcast_to(d, (64, 128))
        return 0

    lax.fori_loop(0, 16, own, 0)
    for t in range(16):
        k_copy(t).wait()

    def cols(p):
        t = jnp.maximum(pt[p], 0)
        return pl.ds(pl.multiple_of(t * UNIT, UNIT), UNIT)

    def crows(p):
        return pl.ds(pl.multiple_of(pc[p] * 256, 256), 256)

    def qk(p, s):
        s[...] = dot_nn(qv[crows(p), :], kt[:, cols(p)])

    def soft(p, s, pr, m, l):
        c, t = pc[p], pt[p]
        base = t * UNIT
        col = lax.broadcasted_iota(jnp.int32, (64, UNIT), 1)
        for k in range(4):
            rr = slice(64 * k, 64 * k + 64)
            lo = jnp.where(t < 0, 1 << 20, starts[c * 4 + k] - base)
            hi = starts[c * 4 + k + 1] - base
            x = jnp.where((col >= lo) & (col < hi), s[rr, :], LOW)
            mx = jnp.max(x, axis=1, keepdims=True)
            e = jnp.exp2((x - mx) * SCALE)
            m[rr, :] = jnp.broadcast_to(mx, (64, 128))
            l[rr, :] = jnp.broadcast_to(jnp.sum(e, axis=1, keepdims=True), (64, 128))
            pr[rr, :] = e.astype(BF16)

    def pv(p, pr, m, l):
        c = pc[p]
        new = (p == 0) | (pc[jnp.maximum(p - 1, 0)] != c)
        o = dot_nt(pr[...], kt[:LAT, cols(p)])
        for k in range(4):
            rr = slice(64 * k, 64 * k + 64)
            r = c * 4 + k
            g = pl.ds(pl.multiple_of(r * 64, 64), 64)
            mo = jnp.where(new, selfs[g, :], mrun[rr, :])
            lo = jnp.where(new, 1.0, lrun[rr, :])
            ao = jnp.where(new, jnp.broadcast_to(latf[pl.ds(r, 1), :LAT], (64, LAT)), acc[rr, :])
            mn = jnp.maximum(mo, m[rr, :])
            al = jnp.exp2((mo - mn) * SCALE)
            be = jnp.exp2((m[rr, :] - mn) * SCALE)
            ln = lo * al + l[rr, :] * be
            an = ao * al[:, :1] + o[rr, :] * be[:, :1]
            mrun[rr, :] = mn
            lrun[rr, :] = ln
            acc[rr, :] = an
            ov[g, :] = (an * (1.0 / ln[:, :1])).astype(BF16)

    qk(0, s0)
    qk(1, s1)
    soft(0, s0, p0, m0, l0)

    def send(c, _):
        o_copy(c).start()
        return 0

    def body(i, done):
        j = 2 * i
        qk(j + 2, s0)
        soft(j + 1, s1, p1, m1, l1)
        pv(j, p0, m0, l0)
        qk(j + 3, s1)
        soft(j + 2, s0, p0, m0, l0)
        pv(j + 1, p1, m1, l1)
        now = pc[j + 2]
        lax.fori_loop(done, now, send, 0)
        return now

    done = lax.fori_loop(0, PAIRS // 2 - 1, body, jnp.int32(0))
    soft(PAIRS - 1, s1, p1, m1, l1)
    pv(PAIRS - 2, p0, m0, l0)
    pv(PAIRS - 1, p1, m1, l1)
    lax.fori_loop(done, 16, send, 0)

    for c in arrivals:
        c.wait()
    writes = []
    for i in range(4):
        ok = i < n
        for j in range(i):
            ok = ok & (req[j] != req[i])
        writes.append(ok)

        @pl.when(ok)
        def _(i=i):
            r = req[i]
            w = jnp.minimum(starts[r] // 128, (4096 - WIN) // 128) * 128
            win = pl.ds(pl.multiple_of(w, 128), WIN)
            rr = pl.ds(pl.multiple_of(r * 64, 64), 64)
            q = qv[rr, :]
            x3 = selfs[rr, :][:, :1]
            x1 = dot_nn(q, kt[:, win])
            col = lax.broadcasted_iota(jnp.int32, (64, WIN), 1) + w
            x1 = jnp.where((col >= starts[r]) & (col < starts[r + 1]), x1, LOW)
            x2 = dot_nt(q, arr[...])
            slot = lax.broadcasted_iota(jnp.int32, (64, 128), 1) // 32
            seen = (slot == 0) & ((0 < n) & (req[0] == r))
            for j in range(1, 4):
                seen = seen | ((slot == j) & ((j < n) & (req[j] == r)))
            x2 = jnp.where(seen, x2, LOW)
            m = jnp.maximum(
                x3,
                jnp.maximum(jnp.max(x1, axis=1, keepdims=True), jnp.max(x2, axis=1, keepdims=True)),
            )
            e1 = jnp.exp2((x1 - m) * SCALE)
            e2 = jnp.exp2((x2 - m) * SCALE)
            e3 = jnp.exp2((x3 - m) * SCALE)
            l = jnp.sum(e1, axis=1, keepdims=True) + jnp.sum(e2, axis=1, keepdims=True) + e3
            o = dot_nt(e1.astype(BF16), kt[:LAT, win]) + dot_nn(e2.astype(BF16), arr[:, :LAT])
            o = o + e3 * latf[pl.ds(r, 1), :LAT]
            ob[i] = (o * (1.0 / l)).astype(BF16)

    for c in range(16):
        o_copy(c).wait()

    def fix_copy(i):
        return pltpu.make_async_copy(
            ob.at[i], out_hbm.at[pl.ds(pl.multiple_of(req[i] * 64, 64), 64), :], fsem.at[i]
        )

    for i in range(4):
        @pl.when(writes[i])
        def _(i=i):
            fix_copy(i).start()

    for i in range(4):
        @pl.when(writes[i])
        def _(i=i):
            fix_copy(i).wait()


def attend_kernel(
    q_hbm, kt_hbm, lat_hbm, len_ref, owner, request, kv_hbm, blk_hbm, out_hbm,
    qv, kv, bias, ps0, ps1, pp0, pp1, pl0, pl1, o0, o1,
    kt, lat, latf, ov, selfs, s0, s1, p0, p1, m0, m1, l0, l1, mrun, lrun, acc, arr, ob,
    starts, pc, pt, req, src, qsem, ksem, lsem, asem, osem, fsem,
):
    side = lax.axis_index("side")

    @pl.when(side == 0)
    def _():
        prefill_side(
            q_hbm, kv_hbm, out_hbm, qv, kv, bias, ps0, ps1, pp0, pp1, pl0, pl1, o0, o1, qsem, ksem, osem
        )

    @pl.when(side == 1)
    def _():
        decode_side(
            q_hbm, kt_hbm, lat_hbm, blk_hbm, len_ref, owner, request, out_hbm,
            qv, kt, lat, latf, ov, selfs, s0, s1, p0, p1, m0, m1, l0, l1, mrun, lrun, acc, arr, ob,
            starts, pc, pt, req, src, qsem, ksem, lsem, asem, osem, fsem,
        )


def attend(q, kt, latent, lengths, owner, request, kv, blocks):
    any_ = pl.BlockSpec(memory_space=pl.ANY)
    smem = pl.BlockSpec(memory_space=pltpu.SMEM)
    v = pltpu.VMEM
    i32 = jnp.int32
    dma = pltpu.SemaphoreType.DMA
    return pl.pallas_call(
        attend_kernel,
        out_shape=jax.ShapeDtypeStruct((VEC, LAT), BF16),
        in_specs=[any_, any_, any_, smem, smem, smem, any_, any_],
        out_specs=any_,
        scratch_shapes=[
            v((VEC, WIDE), BF16), v((2048, WIDE), BF16), v((64, 1024), F32),
            v((BQ, 2048), F32), v((BQ, 2048), F32), v((BQ, 2048), BF16), v((BQ, 2048), BF16),
            v((BQ, 128), F32), v((BQ, 128), F32), v((BQ, LAT), BF16), v((BQ, LAT), BF16),
            v((WIDE, 4096), BF16), v((64, WIDE), BF16), v((64, WIDE), F32), v((VEC, LAT), BF16),
            v((VEC, 128), F32),
            v((256, UNIT), F32), v((256, UNIT), F32), v((256, UNIT), BF16), v((256, UNIT), BF16),
            v((256, 128), F32), v((256, 128), F32), v((256, 128), F32), v((256, 128), F32),
            v((256, 128), F32), v((256, 128), F32), v((256, LAT), F32),
            v((128, WIDE), BF16), v((4, 64, LAT), BF16),
            pltpu.SMEM((65,), i32), pltpu.SMEM((PAIRS,), i32), pltpu.SMEM((PAIRS,), i32),
            pltpu.SMEM((4,), i32), pltpu.SMEM((4,), i32),
            dma((16,)), dma((16,)), dma, dma((4,)), dma((16,)), dma((4,)),
        ],
        compiler_params=pltpu.CompilerParams(vmem_limit_bytes=56 << 20),
        name="attend",
    )(q, kt, latent, lengths, owner, request, kv, blocks)


def local(queries, stream_rows, span_latents, decode_cache, cache_lengths, block_owner, block_request):
    q = queries.reshape(VEC, WIDE)
    stream = stream_rows.reshape(ROWS, WIDE)
    span = span_latents.reshape(ROWS, WIDE)
    owner = block_owner.reshape(128)
    kv, blocks = gather(stream, span, owner)
    out = attend(q, decode_cache.T, stream, cache_lengths, owner, block_request, kv, blocks)
    return out.reshape(1, 1, ROWS, HEADS, LAT)


def solution(mesh):
    return jax.shard_map(
        local,
        mesh=mesh,
        in_specs=(
            P("side", "grp", "seq", None, None),
            P("side", "grp", "seq", None),
            P("grp", "seq", None),
            P(("grp", "seq"), None),
            P(("grp", "seq"), None),
            P(),
            P(),
        ),
        out_specs=P("side", "grp", "seq", None, None),
        check_vma=False,
    )
```

```python
import functools
import math

import jax
import jax.numpy as jnp
from jax import lax
from jax.experimental import pallas as pl
from jax.experimental.pallas import tpu as pltpu
from jax.sharding import PartitionSpec as P

LAT = 512
WIDE = 576
HEADS = 64
ROWS = 64
VEC = ROWS * HEADS
SCALE = 1.4426950408889634 / math.sqrt(192.0)
LOW = -1e30
MESH = pl.DeviceIdType.MESH
F32 = jnp.float32
BF16 = jnp.bfloat16
UNIT = 256
NT = (((1,), (1,)), ((), ()))


def rows(start, size):
    return pl.ds(pl.multiple_of(start, 16), size)


def dot_nt(a, b):
    return lax.dot_general(a, b, NT, preferred_element_type=F32)


def dot_nn(a, b):
    return jnp.dot(a, b, preferred_element_type=F32)


def gather_kernel(
    stream_hbm, span_hbm, owner_hbm, kv_hbm, blk_hbm,
    kv, owner, sendb, recvb, insem, ssem, rsem, dssem, drsem, xssem, xrsem, osem, bsem, wsem,
):
    g = lax.axis_index("grp")
    side = lax.axis_index("side")
    sq = lax.axis_index("seq")
    y, z = sq // 4, sq % 4
    barrier = pltpu.get_barrier_semaphore()

    def device(yy, zz):
        return (yy % 4) * 4 + zz % 4

    @pl.when(side == 0)
    def _():
        for to in [device(y, z + d) for d in (1, 2, 3)] + [device(y + d, z) for d in (1, 2, 3)]:
            pl.semaphore_signal(barrier, inc=1, device_id={"seq": to}, device_id_type=MESH)
        pl.semaphore_signal(barrier, inc=1, device_id={"side": 1}, device_id_type=MESH)

    @pl.when(side == 1)
    def _():
        pl.semaphore_signal(barrier, inc=1, device_id={"side": 0}, device_id_type=MESH)
        for k in range(1, 4):
            pl.semaphore_signal(
                barrier, inc=1, device_id={"grp": (g + k) % 4}, device_id_type=MESH
            )

    def unit_to_decode(u):
        ref = kv.at[rows(u * UNIT, UNIT), :]
        return pltpu.make_async_remote_copy(
            src_ref=ref, dst_ref=ref, send_sem=dssem.at[u], recv_sem=drsem.at[u],
            device_id={"side": 1}, device_id_type=MESH,
        )

    @pl.when(side == 0)
    def _():
        def stream_at(a, b):
            return ((b + 4) % 4) * 256 + ((a + 4) % 4) * 64

        def span_at(a, b):
            return 1024 + ((b + 4) % 4) * 256 + ((a + 4) % 4) * 64

        kinds = (
            (stream_at, z, y, lambda da, db: device(y + db, z + da)),
            (span_at, y, z, lambda da, db: device(y + da, z + db)),
        )
        own = [
            pltpu.make_async_copy(src, kv.at[rows(at(a, b), 64), :], insem.at[n])
            for n, (src, (at, a, b, _)) in enumerate(zip((stream_hbm, span_hbm), kinds))
        ]
        for c in own:
            c.start()
        pl.semaphore_wait(barrier, 7)
        names = {}
        sent = []

        def message(kind, name, start, size, to):
            k = names.setdefault((kind, name), len(names))
            ref = kv.at[rows(start, size), :]
            return pltpu.make_async_remote_copy(
                src_ref=ref, dst_ref=ref, send_sem=ssem.at[k], recv_sem=rsem.at[k],
                device_id={"seq": to}, device_id_type=MESH,
            )

        def send(kind, name, start, size, to):
            c = message(kind, name, start, size, to)
            c.start()
            sent.append(c)

        def take(kind, name, start, size):
            message(kind, name, start, size, sq).wait_recv()

        def both(step):
            for kind in range(2):
                step(kind, *kinds[kind])

        def first(kind, at, a, b, dev):
            own[kind].wait()
            for d in (2, 1, 3):
                send(kind, (0, d), at(a, b), 64, dev(d, 0))
            for d in (2, 1, 3):
                send(kind, (d, 0), at(a, b), 64, dev(0, d))

        def onward(e):
            def step(kind, at, a, b, dev):
                take(kind, (0, e), at(a - e, b), 64)
                for d in (2, 1, 3):
                    send(kind, (d, e), at(a - e, b), 64, dev(0, d))

            return step

        def rest(d):
            def step(kind, at, a, b, dev):
                for e in range(4):
                    take(kind, (d, e), at(a - e, b - d), 64)
                unit_done(kind, (b - d + 4) % 4)

            return step

        def unit_out(u):
            return pltpu.make_async_copy(
                kv.at[rows(u * UNIT, UNIT), :], kv_hbm.at[rows(u * UNIT, UNIT), :], osem.at[u]
            )

        units = []

        def unit_done(kind, u):
            unit_out(u + 4 * kind).start()
            if kind == 0:
                c = unit_to_decode(u)
                c.start()
                units.append(c)

        both(first)
        for e in (1, 3, 2):
            both(onward(e))
        both(lambda kind, at, a, b, dev: unit_done(kind, b))
        for d in (1, 3, 2):
            both(rest(d))
        for u in range(8):
            unit_out(u).wait()
        for c in sent + units:
            c.wait_send()

    @pl.when(side == 1)
    def _():
        names_in = pltpu.make_async_copy(owner_hbm, owner, wsem)
        names_in.start()
        pl.semaphore_wait(barrier, 4)
        names_in.wait()
        lane = lax.broadcasted_iota(jnp.int32, (1, 1024), 1)
        who = [((g + k) % 4) * 16 + sq for k in range(4)]

        def find(b, carry):
            o = owner[g * 32 + b]
            out = []
            for k in range(4):
                n, slots = carry[2 * k], carry[2 * k + 1]
                hit = jnp.where(o == who[k], 1, 0)
                slots = jnp.where(lane // 32 == b, n - (1 - hit) * 8, slots)
                out += [n + hit, slots]
            return tuple(out)

        found = lax.fori_loop(0, 32, find, (jnp.int32(0), jnp.full((1, 1024), -8, jnp.int32)) * 4)
        rowi = lax.broadcasted_iota(jnp.int32, (128, 1024), 0)
        coli = lax.broadcasted_iota(jnp.int32, (128, 1024), 1)
        same = rowi % 32 == coli % 32
        for u in range(4):
            unit_to_decode(u).wait_recv()
        out = []
        for k in (2, 1, 3, 0):
            pick = jnp.where(same & (found[2 * k + 1] == rowi // 32), 1.0, 0.0).astype(BF16)
            sendb[k] = dot_nn(pick, kv[:1024, :]).astype(BF16)
            if k:
                c = pltpu.make_async_remote_copy(
                    src_ref=sendb.at[k], dst_ref=recvb.at[g], send_sem=xssem.at[k],
                    recv_sem=xrsem.at[g], device_id={"grp": (g + k) % 4}, device_id_type=MESH,
                )
            else:
                c = pltpu.make_async_copy(sendb.at[0], blk_hbm.at[g], bsem.at[0])
            c.start()
            out.append(c)
        for k in range(1, 4):
            h = (g + k) % 4
            pltpu.make_async_remote_copy(
                src_ref=sendb.at[k], dst_ref=recvb.at[h], send_sem=xssem.at[k], recv_sem=xrsem.at[h],
                device_id={"grp": h}, device_id_type=MESH,
            ).wait_recv()
            c = pltpu.make_async_copy(recvb.at[h], blk_hbm.at[h], bsem.at[k])
            c.start()
            out.append(c)
        for n, c in enumerate(out):
            if n < 3:
                c.wait_send()
            else:
                c.wait()


def gather(stream, span, owner):
    hbm = pl.BlockSpec(memory_space=pltpu.HBM)
    v = pltpu.VMEM
    dma = pltpu.SemaphoreType.DMA
    return pl.pallas_call(
        gather_kernel,
        out_shape=(
            jax.ShapeDtypeStruct((2048, WIDE), BF16),
            jax.ShapeDtypeStruct((4, 128, WIDE), BF16),
        ),
        in_specs=[hbm, hbm, hbm],
        out_specs=(hbm, hbm),
        scratch_shapes=[
            v((2048, WIDE), BF16), pltpu.SMEM((128,), jnp.int32),
            v((4, 128, WIDE), BF16), v((4, 128, WIDE), BF16),
            dma((2,)), dma((40,)), dma((40,)), dma((4,)), dma((4,)), dma((4,)), dma((4,)), dma((8,)),
            dma((4,)), dma,
        ],
        compiler_params=pltpu.CompilerParams(
            vmem_limit_bytes=32 << 20, collective_id=0, has_side_effects=True
        ),
        name="gather_latents",
    )(stream, span, owner)


PAIRS = 32
BQ = 256
WIN = 384


def prefill_side(q_hbm, kv_hbm, out_hbm, qv, kv, ov, bias, s0, s1, p0, p1, l0, l1, qsem, ksem, osem):
    sq = lax.axis_index("seq")
    nb = VEC // BQ

    def q_copy(i):
        r = rows(i * BQ, BQ)
        return pltpu.make_async_copy(q_hbm.at[r, :], qv.at[r, :], qsem.at[i])

    def k_copy(u):
        r = rows(u * 512, 512)
        return pltpu.make_async_copy(kv_hbm.at[r, :], kv.at[r, :], ksem.at[u])

    q_copy(0).start()
    for u in range(4):
        k_copy(u).start()
    for i in range(1, nb):
        q_copy(i).start()
    row = sq * 64 + lax.broadcasted_iota(jnp.int32, (64, 1024), 0)
    j = lax.broadcasted_iota(jnp.int32, (64, 1024), 1)
    pos = (((j // 64) % 4) * 4 + j // 256) * 64 + j % 64
    bias[...] = jnp.where(pos <= row, 0.0, LOW)

    def scores(i, s):
        q_copy(i).wait()
        s[...] = dot_nt(qv[rows(i * BQ, BQ), :], kv[...])

    def soft(i, s, pr, l):
        xa = s[:, :1024]
        bb = jnp.concatenate([jnp.broadcast_to(bias[pl.ds(i * 4 + k, 1), :], (64, 1024)) for k in range(BQ // 64)], 0)
        xb = s[:, 1024:] + bb
        m = jnp.maximum(jnp.max(xa, axis=1, keepdims=True), jnp.max(xb, axis=1, keepdims=True)) * SCALE
        ea = jnp.exp2(xa * SCALE - m)
        eb = jnp.exp2(xb * SCALE - m)
        pr[:, :1024] = ea.astype(BF16)
        pr[:, 1024:] = eb.astype(BF16)
        t = jnp.sum(ea, axis=1, keepdims=True) + jnp.sum(eb, axis=1, keepdims=True)
        l[...] = jnp.broadcast_to(t, (BQ, 128))

    def out_copy(i):
        r = rows(i * BQ, 2 * BQ)
        return pltpu.make_async_copy(ov.at[r, :], out_hbm.at[r, :], osem.at[i // 2])

    def values(i, pr, l):
        a = dot_nn(pr[...], kv[:, :LAT])
        ov[rows(i * BQ, BQ), :] = (a * (1.0 / l[:, :1])).astype(BF16)

    for u in range(4):
        k_copy(u).wait()
    scores(0, s0)
    scores(1, s1)
    soft(0, s0, p0, l0)

    def body(t, _):
        i = 2 * t
        q_copy(i + 2).wait()
        q_copy(i + 3).wait()
        values(i, p0, l0)
        s0[...] = dot_nt(qv[rows((i + 2) * BQ, BQ), :], kv[...])
        soft(i + 1, s1, p1, l1)
        s1[...] = dot_nt(qv[rows((i + 3) * BQ, BQ), :], kv[...])
        values(i + 1, p1, l1)
        soft(i + 2, s0, p0, l0)
        out_copy(i).start()
        return 0

    lax.fori_loop(0, nb // 2 - 1, body, 0)
    soft(nb - 1, s1, p1, l1)
    values(nb - 2, p0, l0)
    values(nb - 1, p1, l1)
    out_copy(nb - 2).start()
    for t in range(nb // 2):
        out_copy(2 * t).wait()


def decode_side(
    q_hbm, kt_hbm, lat_hbm, blk_hbm, len_ref, owner, request, out_hbm,
    qv, kt, lat, latf, ov, selfs, s0, s1, p0, p1, m0, m1, l0, l1, mrun, lrun, acc, arr, ob,
    starts, pc, pt, req, src, qsem, ksem, lsem, asem, osem, fsem,
):
    me = lax.axis_index("grp") * 16 + lax.axis_index("seq")

    def q_copy(c):
        r = rows(c * 256, 256)
        return pltpu.make_async_copy(q_hbm.at[r, :], qv.at[r, :], qsem.at[c])

    def k_copy(t):
        r = pl.ds(pl.multiple_of(t * 256, 256), 256)
        return pltpu.make_async_copy(kt_hbm.at[:, r], kt.at[:, r], ksem.at[t])

    def o_copy(c):
        r = rows(c * 256, 256)
        return pltpu.make_async_copy(ov.at[r, :], out_hbm.at[r, :], osem.at[c])

    lat_copy = pltpu.make_async_copy(lat_hbm, lat, lsem)
    lat_copy.start()
    for c in range(16):
        q_copy(c).start()
    for t in range(16):
        k_copy(t).start()

    def scan(r, total):
        starts[r] = total
        return total + len_ref[0, r]

    starts[64] = lax.fori_loop(0, 64, scan, jnp.int32(0))

    def fill(p, carry):
        c, t = carry
        pc[p] = jnp.minimum(c, 15)
        pt[p] = jnp.where(c < 16, t, -1)
        cc = jnp.minimum(c, 15)
        more = (t + 1) * UNIT < starts[cc * 4 + 4]
        nc = jnp.where(more, c, c + 1)
        ns = starts[jnp.minimum(nc, 15) * 4]
        nt = jnp.where(more, t + 1, ns // UNIT)
        return nc, nt

    lax.fori_loop(0, PAIRS, fill, (jnp.int32(0), jnp.int32(0)))
    for i in range(4):
        req[i] = 0
        src[i] = 0

    def find(b, carry):
        n, rank = carry
        rank = jnp.where(b % 32 == 0, 0, rank)
        hit = owner[b] == me

        @pl.when(hit)
        def _():
            req[n] = request[b]
            src[n] = (b // 32) * 4 + rank

        h = hit.astype(jnp.int32)
        return n + h, rank + h

    n, _ = lax.fori_loop(0, 128, find, (jnp.int32(0), jnp.int32(0)))
    arrivals = []
    for i in range(4):
        s = src[i]
        arrivals.append(
            pltpu.make_async_copy(
                blk_hbm.at[s // 4, pl.ds(pl.multiple_of((s % 4) * 32, 32), 32), :],
                arr.at[pl.ds(32 * i, 32), :], asem.at[i],
            )
        )
    for c in arrivals:
        c.start()
    lat_copy.wait()
    latf[...] = lat[...].astype(F32)

    def own(c, _):
        q_copy(c).wait()
        for k in range(4):
            r = c * 4 + k
            rr = pl.ds(pl.multiple_of(r * 64, 64), 64)
            d = jnp.sum(qv[rr, :].astype(F32) * latf[pl.ds(r, 1), :], axis=1, keepdims=True)
            selfs[rr, :] = jnp.broadcast_to(d, (64, 128))
        return 0

    lax.fori_loop(0, 16, own, 0)
    for t in range(16):
        k_copy(t).wait()

    def cols(p):
        t = jnp.maximum(pt[p], 0)
        return pl.ds(pl.multiple_of(t * UNIT, UNIT), UNIT)

    def crows(p):
        return pl.ds(pl.multiple_of(pc[p] * 256, 256), 256)

    def qk(p, s):
        s[...] = dot_nn(qv[crows(p), :], kt[:, cols(p)])

    def soft(p, s, pr, m, l):
        c, t = pc[p], pt[p]
        base = t * UNIT
        col = lax.broadcasted_iota(jnp.int32, (64, UNIT), 1)
        for k in range(4):
            rr = slice(64 * k, 64 * k + 64)
            lo = jnp.where(t < 0, 1 << 20, starts[c * 4 + k] - base)
            hi = starts[c * 4 + k + 1] - base
            x = jnp.where((col >= lo) & (col < hi), s[rr, :], LOW)
            mx = jnp.max(x, axis=1, keepdims=True)
            e = jnp.exp2((x - mx) * SCALE)
            m[rr, :] = jnp.broadcast_to(mx, (64, 128))
            l[rr, :] = jnp.broadcast_to(jnp.sum(e, axis=1, keepdims=True), (64, 128))
            pr[rr, :] = e.astype(BF16)

    def pv(p, pr, m, l):
        c = pc[p]
        new = (p == 0) | (pc[jnp.maximum(p - 1, 0)] != c)
        o = dot_nt(pr[...], kt[:LAT, cols(p)])
        for k in range(4):
            rr = slice(64 * k, 64 * k + 64)
            r = c * 4 + k
            g = pl.ds(pl.multiple_of(r * 64, 64), 64)
            mo = jnp.where(new, selfs[g, :], mrun[rr, :])
            lo = jnp.where(new, 1.0, lrun[rr, :])
            ao = jnp.where(new, jnp.broadcast_to(latf[pl.ds(r, 1), :LAT], (64, LAT)), acc[rr, :])
            mn = jnp.maximum(mo, m[rr, :])
            al = jnp.exp2((mo - mn) * SCALE)
            be = jnp.exp2((m[rr, :] - mn) * SCALE)
            ln = lo * al + l[rr, :] * be
            an = ao * al[:, :1] + o[rr, :] * be[:, :1]
            mrun[rr, :] = mn
            lrun[rr, :] = ln
            acc[rr, :] = an
            ov[g, :] = (an * (1.0 / ln[:, :1])).astype(BF16)

    qk(0, s0)
    qk(1, s1)
    soft(0, s0, p0, m0, l0)

    def send(c, _):
        o_copy(c).start()
        return 0

    def body(i, done):
        j = 2 * i
        qk(j + 2, s0)
        soft(j + 1, s1, p1, m1, l1)
        pv(j, p0, m0, l0)
        qk(j + 3, s1)
        soft(j + 2, s0, p0, m0, l0)
        pv(j + 1, p1, m1, l1)
        now = pc[j + 2]
        lax.fori_loop(done, now, send, 0)
        return now

    done = lax.fori_loop(0, PAIRS // 2 - 1, body, jnp.int32(0))
    soft(PAIRS - 1, s1, p1, m1, l1)
    pv(PAIRS - 2, p0, m0, l0)
    pv(PAIRS - 1, p1, m1, l1)
    lax.fori_loop(done, 16, send, 0)

    for c in arrivals:
        c.wait()
    writes = []
    for i in range(4):
        ok = i < n
        for j in range(i):
            ok = ok & (req[j] != req[i])
        writes.append(ok)

        @pl.when(ok)
        def _(i=i):
            r = req[i]
            w = jnp.minimum(starts[r] // 128, (4096 - WIN) // 128) * 128
            win = pl.ds(pl.multiple_of(w, 128), WIN)
            rr = pl.ds(pl.multiple_of(r * 64, 64), 64)
            q = qv[rr, :]
            x3 = selfs[rr, :][:, :1]
            x1 = dot_nn(q, kt[:, win])
            col = lax.broadcasted_iota(jnp.int32, (64, WIN), 1) + w
            x1 = jnp.where((col >= starts[r]) & (col < starts[r + 1]), x1, LOW)
            x2 = dot_nt(q, arr[...])
            slot = lax.broadcasted_iota(jnp.int32, (64, 128), 1) // 32
            seen = (slot == 0) & ((0 < n) & (req[0] == r))
            for j in range(1, 4):
                seen = seen | ((slot == j) & ((j < n) & (req[j] == r)))
            x2 = jnp.where(seen, x2, LOW)
            m = jnp.maximum(
                x3,
                jnp.maximum(jnp.max(x1, axis=1, keepdims=True), jnp.max(x2, axis=1, keepdims=True)),
            )
            e1 = jnp.exp2((x1 - m) * SCALE)
            e2 = jnp.exp2((x2 - m) * SCALE)
            e3 = jnp.exp2((x3 - m) * SCALE)
            l = jnp.sum(e1, axis=1, keepdims=True) + jnp.sum(e2, axis=1, keepdims=True) + e3
            o = dot_nt(e1.astype(BF16), kt[:LAT, win]) + dot_nn(e2.astype(BF16), arr[:, :LAT])
            o = o + e3 * latf[pl.ds(r, 1), :LAT]
            ob[i] = (o * (1.0 / l)).astype(BF16)

    for c in range(16):
        o_copy(c).wait()

    def fix_copy(i):
        return pltpu.make_async_copy(
            ob.at[i], out_hbm.at[pl.ds(pl.multiple_of(req[i] * 64, 64), 64), :], fsem.at[i]
        )

    for i in range(4):
        @pl.when(writes[i])
        def _(i=i):
            fix_copy(i).start()

    for i in range(4):
        @pl.when(writes[i])
        def _(i=i):
            fix_copy(i).wait()


def attend_kernel(
    q_hbm, kt_hbm, lat_hbm, len_hbm, owner_hbm, request_hbm, kv_hbm, blk_hbm, out_hbm,
    qv, kv, bias, ps0, ps1, pp0, pp1, pl0, pl1,
    kt, lat, latf, ov, selfs, s0, s1, p0, p1, m0, m1, l0, l1, mrun, lrun, acc, arr, ob,
    starts, pc, pt, req, src, len_ref, owner, request, qsem, ksem, lsem, asem, osem, fsem, isem,
):
    side = lax.axis_index("side")

    @pl.when(side == 0)
    def _():
        prefill_side(
            q_hbm, kv_hbm, out_hbm, qv, kv, ov, bias, ps0, ps1, pp0, pp1, pl0, pl1, qsem, ksem, osem
        )

    @pl.when(side == 1)
    def _():
        small = [
            pltpu.make_async_copy(a, b, isem.at[n])
            for n, (a, b) in enumerate(
                ((len_hbm, len_ref), (owner_hbm, owner), (request_hbm, request))
            )
        ]
        for c in small:
            c.start()
        for c in small:
            c.wait()
        decode_side(
            q_hbm, kt_hbm, lat_hbm, blk_hbm, len_ref, owner, request, out_hbm,
            qv, kt, lat, latf, ov, selfs, s0, s1, p0, p1, m0, m1, l0, l1, mrun, lrun, acc, arr, ob,
            starts, pc, pt, req, src, qsem, ksem, lsem, asem, osem, fsem,
        )


def attend(q, kt, latent, lengths, owner, request, kv, blocks):
    any_ = pl.BlockSpec(memory_space=pltpu.HBM)
    v = pltpu.VMEM
    i32 = jnp.int32
    dma = pltpu.SemaphoreType.DMA
    return pl.pallas_call(
        attend_kernel,
        out_shape=jax.ShapeDtypeStruct((VEC, LAT), BF16),
        in_specs=[any_] * 8,
        out_specs=any_,
        scratch_shapes=[
            v((VEC, WIDE), BF16), v((2048, WIDE), BF16), v((64, 1024), F32),
            v((BQ, 2048), F32), v((BQ, 2048), F32), v((BQ, 2048), BF16), v((BQ, 2048), BF16),
            v((BQ, 128), F32), v((BQ, 128), F32),
            v((WIDE, 4096), BF16), v((64, WIDE), BF16), v((64, WIDE), F32), v((VEC, LAT), BF16),
            v((VEC, 128), F32),
            v((256, UNIT), F32), v((256, UNIT), F32), v((256, UNIT), BF16), v((256, UNIT), BF16),
            v((256, 128), F32), v((256, 128), F32), v((256, 128), F32), v((256, 128), F32),
            v((256, 128), F32), v((256, 128), F32), v((256, LAT), F32),
            v((128, WIDE), BF16), v((4, 64, LAT), BF16),
            pltpu.SMEM((65,), i32), pltpu.SMEM((PAIRS,), i32), pltpu.SMEM((PAIRS,), i32),
            pltpu.SMEM((4,), i32), pltpu.SMEM((4,), i32),
            pltpu.SMEM((1, 64), i32), pltpu.SMEM((128,), i32), pltpu.SMEM((128,), i32),
            dma((16,)), dma((16,)), dma, dma((4,)), dma((16,)), dma((4,)), dma((3,)),
        ],
        compiler_params=pltpu.CompilerParams(vmem_limit_bytes=56 << 20),
        name="attend",
    )(q, kt, latent, lengths, owner, request, kv, blocks)


def local(queries, stream_rows, span_latents, decode_cache, cache_lengths, block_owner, block_request):
    q = queries.reshape(VEC, WIDE)
    stream = stream_rows.reshape(ROWS, WIDE)
    span = span_latents.reshape(ROWS, WIDE)
    owner = block_owner.reshape(128)
    kv, blocks = gather(stream, span, owner)
    out = attend(q, decode_cache.T, stream, cache_lengths, owner, block_request, kv, blocks)
    return out.reshape(1, 1, ROWS, HEADS, LAT)


def solution(mesh):
    return jax.shard_map(
        local,
        mesh=mesh,
        in_specs=(
            P("side", "grp", "seq", None, None),
            P("side", "grp", "seq", None),
            P("grp", "seq", None),
            P(("grp", "seq"), None),
            P(("grp", "seq"), None),
            P(),
            P(),
        ),
        out_specs=P("side", "grp", "seq", None, None),
        check_vma=False,
    )
```

```python
import functools
import math

import jax
import jax.numpy as jnp
from jax import lax
from jax.experimental import pallas as pl
from jax.experimental.pallas import tpu as pltpu
from jax.sharding import PartitionSpec as P

LAT = 512
WIDE = 576
HEADS = 64
ROWS = 64
VEC = ROWS * HEADS
SCALE = 1.4426950408889634 / math.sqrt(192.0)
LOW = -1e30
MESH = pl.DeviceIdType.MESH
F32 = jnp.float32
BF16 = jnp.bfloat16
UNIT = 256
NT = (((1,), (1,)), ((), ()))


def rows(start, size):
    return pl.ds(pl.multiple_of(start, 16), size)


def dot_nt(a, b):
    return lax.dot_general(a, b, NT, preferred_element_type=F32)


def dot_nn(a, b):
    return jnp.dot(a, b, preferred_element_type=F32)


def gather_kernel(
    stream_hbm, span_hbm, owner_hbm, kv_hbm, blk_hbm,
    kv, owner, sendb, recvb, insem, ssem, rsem, dssem, drsem, xssem, xrsem, osem, bsem, wsem,
):
    g = lax.axis_index("grp")
    side = lax.axis_index("side")
    sq = lax.axis_index("seq")
    y, z = sq // 4, sq % 4
    barrier = pltpu.get_barrier_semaphore()

    def device(yy, zz):
        return (yy % 4) * 4 + zz % 4

    @pl.when(side == 0)
    def _():
        for to in [device(y, z + d) for d in (1, 2, 3)] + [device(y + d, z) for d in (1, 2, 3)]:
            pl.semaphore_signal(barrier, inc=1, device_id={"seq": to}, device_id_type=MESH)
        pl.semaphore_signal(barrier, inc=1, device_id={"side": 1}, device_id_type=MESH)

    @pl.when(side == 1)
    def _():
        pl.semaphore_signal(barrier, inc=1, device_id={"side": 0}, device_id_type=MESH)
        for k in range(1, 4):
            pl.semaphore_signal(
                barrier, inc=1, device_id={"grp": (g + k) % 4}, device_id_type=MESH
            )

    def unit_to_decode(u):
        ref = kv.at[rows(u * UNIT, UNIT), :]
        return pltpu.make_async_remote_copy(
            src_ref=ref, dst_ref=ref, send_sem=dssem.at[u], recv_sem=drsem.at[u],
            device_id={"side": 1}, device_id_type=MESH,
        )

    @pl.when(side == 0)
    def _():
        def stream_at(a, b):
            return ((b + 4) % 4) * 256 + ((a + 4) % 4) * 64

        def span_at(a, b):
            return 1024 + ((b + 4) % 4) * 256 + ((a + 4) % 4) * 64

        kinds = (
            (stream_at, z, y, lambda da, db: device(y + db, z + da)),
            (span_at, y, z, lambda da, db: device(y + da, z + db)),
        )
        own = [
            pltpu.make_async_copy(src, kv.at[rows(at(a, b), 64), :], insem.at[n])
            for n, (src, (at, a, b, _)) in enumerate(zip((stream_hbm, span_hbm), kinds))
        ]
        for c in own:
            c.start()
        pl.semaphore_wait(barrier, 7)
        names = {}
        sent = []

        def message(kind, name, start, size, to):
            k = names.setdefault((kind, name), len(names))
            ref = kv.at[rows(start, size), :]
            return pltpu.make_async_remote_copy(
                src_ref=ref, dst_ref=ref, send_sem=ssem.at[k], recv_sem=rsem.at[k],
                device_id={"seq": to}, device_id_type=MESH,
            )

        def send(kind, name, start, size, to):
            c = message(kind, name, start, size, to)
            c.start()
            sent.append(c)

        def take(kind, name, start, size):
            message(kind, name, start, size, sq).wait_recv()

        def both(step):
            for kind in range(2):
                step(kind, *kinds[kind])

        def first(kind, at, a, b, dev):
            own[kind].wait()
            for d in (2, 1, 3):
                send(kind, (0, d), at(a, b), 64, dev(d, 0))
            for d in (2, 1, 3):
                send(kind, (d, 0), at(a, b), 64, dev(0, d))

        def onward(e):
            def step(kind, at, a, b, dev):
                take(kind, (0, e), at(a - e, b), 64)
                for d in (2, 1, 3):
                    send(kind, (d, e), at(a - e, b), 64, dev(0, d))

            return step

        def rest(d):
            def step(kind, at, a, b, dev):
                for e in range(4):
                    take(kind, (d, e), at(a - e, b - d), 64)
                unit_done(kind, (b - d + 4) % 4)

            return step

        def unit_out(u):
            return pltpu.make_async_copy(
                kv.at[rows(u * UNIT, UNIT), :], kv_hbm.at[rows(u * UNIT, UNIT), :], osem.at[u]
            )

        units = []

        def unit_done(kind, u):
            unit_out(u + 4 * kind).start()
            if kind == 0:
                c = unit_to_decode(u)
                c.start()
                units.append(c)

        both(first)
        for e in (1, 3, 2):
            both(onward(e))
        both(lambda kind, at, a, b, dev: unit_done(kind, b))
        for d in (1, 3, 2):
            both(rest(d))
        for u in range(8):
            unit_out(u).wait()
        for c in sent + units:
            c.wait_send()

    @pl.when(side == 1)
    def _():
        names_in = pltpu.make_async_copy(owner_hbm, owner, wsem)
        names_in.start()
        pl.semaphore_wait(barrier, 4)
        names_in.wait()
        lane = lax.broadcasted_iota(jnp.int32, (1, 1024), 1)
        who = [((g + k) % 4) * 16 + sq for k in range(4)]

        def find(b, carry):
            o = owner[g * 32 + b]
            out = []
            for k in range(4):
                n, slots = carry[2 * k], carry[2 * k + 1]
                hit = jnp.where(o == who[k], 1, 0)
                slots = jnp.where(lane // 32 == b, n - (1 - hit) * 8, slots)
                out += [n + hit, slots]
            return tuple(out)

        found = lax.fori_loop(0, 32, find, (jnp.int32(0), jnp.full((1, 1024), -8, jnp.int32)) * 4)
        rowi = lax.broadcasted_iota(jnp.int32, (128, 1024), 0)
        coli = lax.broadcasted_iota(jnp.int32, (128, 1024), 1)
        same = rowi % 32 == coli % 32
        for u in range(4):
            unit_to_decode(u).wait_recv()
        out = []
        for k in (2, 1, 3, 0):
            pick = jnp.where(same & (found[2 * k + 1] == rowi // 32), 1.0, 0.0).astype(BF16)
            sendb[k] = dot_nn(pick, kv[:1024, :]).astype(BF16)
            if k:
                c = pltpu.make_async_remote_copy(
                    src_ref=sendb.at[k], dst_ref=recvb.at[g], send_sem=xssem.at[k],
                    recv_sem=xrsem.at[g], device_id={"grp": (g + k) % 4}, device_id_type=MESH,
                )
            else:
                c = pltpu.make_async_copy(sendb.at[0], blk_hbm.at[g], bsem.at[0])
            c.start()
            out.append(c)
        for k in range(1, 4):
            h = (g + k) % 4
            pltpu.make_async_remote_copy(
                src_ref=sendb.at[k], dst_ref=recvb.at[h], send_sem=xssem.at[k], recv_sem=xrsem.at[h],
                device_id={"grp": h}, device_id_type=MESH,
            ).wait_recv()
            c = pltpu.make_async_copy(recvb.at[h], blk_hbm.at[h], bsem.at[k])
            c.start()
            out.append(c)
        for n, c in enumerate(out):
            if n < 3:
                c.wait_send()
            else:
                c.wait()


def gather(stream, span, owner):
    hbm = pl.BlockSpec(memory_space=pltpu.HBM)
    v = pltpu.VMEM
    dma = pltpu.SemaphoreType.DMA
    return pl.pallas_call(
        gather_kernel,
        out_shape=(
            jax.ShapeDtypeStruct((2048, WIDE), BF16),
            jax.ShapeDtypeStruct((4, 128, WIDE), BF16),
        ),
        in_specs=[hbm, hbm, hbm],
        out_specs=(hbm, hbm),
        scratch_shapes=[
            v((2048, WIDE), BF16), pltpu.SMEM((128,), jnp.int32),
            v((4, 128, WIDE), BF16), v((4, 128, WIDE), BF16),
            dma((2,)), dma((40,)), dma((40,)), dma((4,)), dma((4,)), dma((4,)), dma((4,)), dma((8,)),
            dma((4,)), dma,
        ],
        compiler_params=pltpu.CompilerParams(
            vmem_limit_bytes=60 << 20, collective_id=0, has_side_effects=True
        ),
        name="gather_latents",
    )(stream, span, owner)


PAIRS = 32
BQ = 256
WIN = 384


def prefill_side(q_hbm, kv_hbm, out_hbm, qv, kv, ov, bias, s0, s1, p0, p1, l0, l1, qsem, ksem, osem):
    sq = lax.axis_index("seq")
    nb = VEC // BQ

    def q_copy(i):
        r = rows(i * BQ, BQ)
        return pltpu.make_async_copy(q_hbm.at[r, :], qv.at[r, :], qsem.at[i])

    def k_copy(u):
        r = rows(u * 512, 512)
        return pltpu.make_async_copy(kv_hbm.at[r, :], kv.at[r, :], ksem.at[u])

    q_copy(0).start()
    for u in range(4):
        k_copy(u).start()
    for i in range(1, nb):
        q_copy(i).start()
    row = sq * 64 + lax.broadcasted_iota(jnp.int32, (64, 1024), 0)
    j = lax.broadcasted_iota(jnp.int32, (64, 1024), 1)
    pos = (((j // 64) % 4) * 4 + j // 256) * 64 + j % 64
    bias[...] = jnp.where(pos <= row, 0.0, LOW)

    parts = 4
    kc, rc = 2048 // parts, BQ // parts

    def scores(i, s, c):
        keys = slice(kc * c, kc * c + kc)
        s[:, keys] = dot_nt(qv[rows(i * BQ, BQ), :], kv[keys, :])

    def soft(i, s, pr, l, c):
        r = slice(rc * c, rc * c + rc)
        xa = s[r, :1024]
        xb = s[r, 1024:] + bias[pl.ds(i * 4 + (rc * c) // 64, 1), :]
        m = jnp.maximum(jnp.max(xa, axis=1, keepdims=True), jnp.max(xb, axis=1, keepdims=True)) * SCALE
        ea = jnp.exp2(xa * SCALE - m)
        eb = jnp.exp2(xb * SCALE - m)
        pr[r, :1024] = ea.astype(BF16)
        pr[r, 1024:] = eb.astype(BF16)
        t = jnp.sum(ea, axis=1, keepdims=True) + jnp.sum(eb, axis=1, keepdims=True)
        l[r, :] = jnp.broadcast_to(t, (rc, 128))

    def out_copy(i):
        r = rows(i * BQ, 2 * BQ)
        return pltpu.make_async_copy(ov.at[r, :], out_hbm.at[r, :], osem.at[i // 2])

    def values(i, pr, l, h):
        cols = slice(256 * h, 256 * h + 256)
        a = dot_nn(pr[...], kv[:, cols])
        ov[rows(i * BQ, BQ), cols] = (a * (1.0 / l[:, :1])).astype(BF16)

    q_copy(0).wait()
    for c in range(parts):
        k_copy(c).wait()
        scores(0, s0, c)
    q_copy(1).wait()
    for c in range(parts):
        scores(1, s1, c)
        soft(0, s0, p0, l0, c)

    def half(i, sa, sb, pa, pb, la, lb):
        for c in range(parts):
            scores(i + 2, sa, c)
            soft(i + 1, sb, pb, lb, c)
            if c == parts // 2 - 1:
                values(i, pa, la, 0)
        values(i, pa, la, 1)

    def body(t, _):
        i = 2 * t
        q_copy(i + 2).wait()
        q_copy(i + 3).wait()
        half(i, s0, s1, p0, p1, l0, l1)
        half(i + 1, s1, s0, p1, p0, l1, l0)
        out_copy(i).start()
        return 0

    lax.fori_loop(0, nb // 2 - 1, body, 0)
    for c in range(parts):
        soft(nb - 1, s1, p1, l1, c)
    for h in range(2):
        values(nb - 2, p0, l0, h)
    for h in range(2):
        values(nb - 1, p1, l1, h)
    out_copy(nb - 2).start()
    for t in range(nb // 2):
        out_copy(2 * t).wait()


def decode_side(
    q_hbm, kt_hbm, lat_hbm, blk_hbm, len_ref, owner, request, out_hbm,
    qv, kt, lat, latf, ov, selfs, s0, s1, p0, p1, m0, m1, l0, l1, mrun, lrun, acc, arr, ob,
    starts, pc, pt, req, src, qsem, ksem, lsem, asem, osem, fsem,
):
    me = lax.axis_index("grp") * 16 + lax.axis_index("seq")

    def q_copy(c):
        r = rows(c * 256, 256)
        return pltpu.make_async_copy(q_hbm.at[r, :], qv.at[r, :], qsem.at[c])

    def k_copy(t):
        r = pl.ds(pl.multiple_of(t * 256, 256), 256)
        return pltpu.make_async_copy(kt_hbm.at[:, r], kt.at[:, r], ksem.at[t])

    def o_copy(c):
        r = rows(c * 256, 256)
        return pltpu.make_async_copy(ov.at[r, :], out_hbm.at[r, :], osem.at[c])

    lat_copy = pltpu.make_async_copy(lat_hbm, lat, lsem)
    lat_copy.start()
    for c in range(16):
        q_copy(c).start()
    for t in range(16):
        k_copy(t).start()

    def scan(r, total):
        starts[r] = total
        return total + len_ref[0, r]

    starts[64] = lax.fori_loop(0, 64, scan, jnp.int32(0))

    def fill(p, carry):
        c, t = carry
        pc[p] = jnp.minimum(c, 15)
        pt[p] = jnp.where(c < 16, t, -1)
        cc = jnp.minimum(c, 15)
        more = (t + 1) * UNIT < starts[cc * 4 + 4]
        nc = jnp.where(more, c, c + 1)
        ns = starts[jnp.minimum(nc, 15) * 4]
        nt = jnp.where(more, t + 1, ns // UNIT)
        return nc, nt

    lax.fori_loop(0, PAIRS, fill, (jnp.int32(0), jnp.int32(0)))
    for i in range(4):
        req[i] = 0
        src[i] = 0

    def find(b, carry):
        n, rank = carry
        rank = jnp.where(b % 32 == 0, 0, rank)
        hit = owner[b] == me

        @pl.when(hit)
        def _():
            req[n] = request[b]
            src[n] = (b // 32) * 4 + rank

        h = hit.astype(jnp.int32)
        return n + h, rank + h

    n, _ = lax.fori_loop(0, 128, find, (jnp.int32(0), jnp.int32(0)))
    arrivals = []
    for i in range(4):
        s = src[i]
        arrivals.append(
            pltpu.make_async_copy(
                blk_hbm.at[s // 4, pl.ds(pl.multiple_of((s % 4) * 32, 32), 32), :],
                arr.at[pl.ds(32 * i, 32), :], asem.at[i],
            )
        )
    for c in arrivals:
        c.start()
    lat_copy.wait()
    latf[...] = lat[...].astype(F32)

    def own(c, _):
        q_copy(c).wait()
        for k in range(4):
            r = c * 4 + k
            rr = pl.ds(pl.multiple_of(r * 64, 64), 64)
            d = jnp.sum(qv[rr, :].astype(F32) * latf[pl.ds(r, 1), :], axis=1, keepdims=True)
            selfs[rr, :] = jnp.broadcast_to(d, (64, 128))
        return 0

    lax.fori_loop(0, 16, own, 0)
    for t in range(16):
        k_copy(t).wait()

    def cols(p):
        t = jnp.maximum(pt[p], 0)
        return pl.ds(pl.multiple_of(t * UNIT, UNIT), UNIT)

    def crows(p):
        return pl.ds(pl.multiple_of(pc[p] * 256, 256), 256)

    def qk(p, s):
        s[...] = dot_nn(qv[crows(p), :], kt[:, cols(p)])

    def soft(p, s, pr, m, l):
        c, t = pc[p], pt[p]
        base = t * UNIT
        col = lax.broadcasted_iota(jnp.int32, (64, UNIT), 1)
        for k in range(4):
            rr = slice(64 * k, 64 * k + 64)
            lo = jnp.where(t < 0, 1 << 20, starts[c * 4 + k] - base)
            hi = starts[c * 4 + k + 1] - base
            x = jnp.where((col >= lo) & (col < hi), s[rr, :], LOW)
            mx = jnp.max(x, axis=1, keepdims=True)
            e = jnp.exp2((x - mx) * SCALE)
            m[rr, :] = jnp.broadcast_to(mx, (64, 128))
            l[rr, :] = jnp.broadcast_to(jnp.sum(e, axis=1, keepdims=True), (64, 128))
            pr[rr, :] = e.astype(BF16)

    def pv(p, pr, m, l):
        c = pc[p]
        new = (p == 0) | (pc[jnp.maximum(p - 1, 0)] != c)
        o = dot_nt(pr[...], kt[:LAT, cols(p)])
        for k in range(4):
            rr = slice(64 * k, 64 * k + 64)
            r = c * 4 + k
            g = pl.ds(pl.multiple_of(r * 64, 64), 64)
            mo = jnp.where(new, selfs[g, :], mrun[rr, :])
            lo = jnp.where(new, 1.0, lrun[rr, :])
            ao = jnp.where(new, jnp.broadcast_to(latf[pl.ds(r, 1), :LAT], (64, LAT)), acc[rr, :])
            mn = jnp.maximum(mo, m[rr, :])
            al = jnp.exp2((mo - mn) * SCALE)
            be = jnp.exp2((m[rr, :] - mn) * SCALE)
            ln = lo * al + l[rr, :] * be
            an = ao * al[:, :1] + o[rr, :] * be[:, :1]
            mrun[rr, :] = mn
            lrun[rr, :] = ln
            acc[rr, :] = an
            ov[g, :] = (an * (1.0 / ln[:, :1])).astype(BF16)

    qk(0, s0)
    qk(1, s1)
    soft(0, s0, p0, m0, l0)

    def send(c, _):
        o_copy(c).start()
        return 0

    def body(i, done):
        j = 2 * i
        qk(j + 2, s0)
        soft(j + 1, s1, p1, m1, l1)
        pv(j, p0, m0, l0)
        qk(j + 3, s1)
        soft(j + 2, s0, p0, m0, l0)
        pv(j + 1, p1, m1, l1)
        now = pc[j + 2]
        lax.fori_loop(done, now, send, 0)
        return now

    done = lax.fori_loop(0, PAIRS // 2 - 1, body, jnp.int32(0))
    soft(PAIRS - 1, s1, p1, m1, l1)
    pv(PAIRS - 2, p0, m0, l0)
    pv(PAIRS - 1, p1, m1, l1)
    lax.fori_loop(done, 16, send, 0)

    for c in arrivals:
        c.wait()
    writes = []
    for i in range(4):
        ok = i < n
        for j in range(i):
            ok = ok & (req[j] != req[i])
        writes.append(ok)

        @pl.when(ok)
        def _(i=i):
            r = req[i]
            w = jnp.minimum(starts[r] // 128, (4096 - WIN) // 128) * 128
            win = pl.ds(pl.multiple_of(w, 128), WIN)
            rr = pl.ds(pl.multiple_of(r * 64, 64), 64)
            q = qv[rr, :]
            x3 = selfs[rr, :][:, :1]
            x1 = dot_nn(q, kt[:, win])
            col = lax.broadcasted_iota(jnp.int32, (64, WIN), 1) + w
            x1 = jnp.where((col >= starts[r]) & (col < starts[r + 1]), x1, LOW)
            x2 = dot_nt(q, arr[...])
            slot = lax.broadcasted_iota(jnp.int32, (64, 128), 1) // 32
            seen = (slot == 0) & ((0 < n) & (req[0] == r))
            for j in range(1, 4):
                seen = seen | ((slot == j) & ((j < n) & (req[j] == r)))
            x2 = jnp.where(seen, x2, LOW)
            m = jnp.maximum(
                x3,
                jnp.maximum(jnp.max(x1, axis=1, keepdims=True), jnp.max(x2, axis=1, keepdims=True)),
            )
            e1 = jnp.exp2((x1 - m) * SCALE)
            e2 = jnp.exp2((x2 - m) * SCALE)
            e3 = jnp.exp2((x3 - m) * SCALE)
            l = jnp.sum(e1, axis=1, keepdims=True) + jnp.sum(e2, axis=1, keepdims=True) + e3
            o = dot_nt(e1.astype(BF16), kt[:LAT, win]) + dot_nn(e2.astype(BF16), arr[:, :LAT])
            o = o + e3 * latf[pl.ds(r, 1), :LAT]
            ob[i] = (o * (1.0 / l)).astype(BF16)

    for c in range(16):
        o_copy(c).wait()

    def fix_copy(i):
        return pltpu.make_async_copy(
            ob.at[i], out_hbm.at[pl.ds(pl.multiple_of(req[i] * 64, 64), 64), :], fsem.at[i]
        )

    for i in range(4):
        @pl.when(writes[i])
        def _(i=i):
            fix_copy(i).start()

    for i in range(4):
        @pl.when(writes[i])
        def _(i=i):
            fix_copy(i).wait()


def attend_kernel(
    q_hbm, kt_hbm, lat_hbm, len_hbm, owner_hbm, request_hbm, kv_hbm, blk_hbm, out_hbm,
    qv, kv, bias, ps0, ps1, pp0, pp1, pl0, pl1,
    kt, lat, latf, ov, selfs, s0, s1, p0, p1, m0, m1, l0, l1, mrun, lrun, acc, arr, ob,
    starts, pc, pt, req, src, len_ref, owner, request, qsem, ksem, lsem, asem, osem, fsem, isem,
):
    side = lax.axis_index("side")

    @pl.when(side == 0)
    def _():
        prefill_side(
            q_hbm, kv_hbm, out_hbm, qv, kv, ov, bias, ps0, ps1, pp0, pp1, pl0, pl1, qsem, ksem, osem
        )

    @pl.when(side == 1)
    def _():
        small = [
            pltpu.make_async_copy(a, b, isem.at[n])
            for n, (a, b) in enumerate(
                ((len_hbm, len_ref), (owner_hbm, owner), (request_hbm, request))
            )
        ]
        for c in small:
            c.start()
        for c in small:
            c.wait()
        decode_side(
            q_hbm, kt_hbm, lat_hbm, blk_hbm, len_ref, owner, request, out_hbm,
            qv, kt, lat, latf, ov, selfs, s0, s1, p0, p1, m0, m1, l0, l1, mrun, lrun, acc, arr, ob,
            starts, pc, pt, req, src, qsem, ksem, lsem, asem, osem, fsem,
        )


def attend(q, kt, latent, lengths, owner, request, kv, blocks):
    any_ = pl.BlockSpec(memory_space=pltpu.HBM)
    v = pltpu.VMEM
    i32 = jnp.int32
    dma = pltpu.SemaphoreType.DMA
    return pl.pallas_call(
        attend_kernel,
        out_shape=jax.ShapeDtypeStruct((VEC, LAT), BF16),
        in_specs=[any_] * 8,
        out_specs=any_,
        scratch_shapes=[
            v((VEC, WIDE), BF16), v((2048, WIDE), BF16), v((64, 1024), F32),
            v((BQ, 2048), F32), v((BQ, 2048), F32), v((BQ, 2048), BF16), v((BQ, 2048), BF16),
            v((BQ, 128), F32), v((BQ, 128), F32),
            v((WIDE, 4096), BF16), v((64, WIDE), BF16), v((64, WIDE), F32), v((VEC, LAT), BF16),
            v((VEC, 128), F32),
            v((256, UNIT), F32), v((256, UNIT), F32), v((256, UNIT), BF16), v((256, UNIT), BF16),
            v((256, 128), F32), v((256, 128), F32), v((256, 128), F32), v((256, 128), F32),
            v((256, 128), F32), v((256, 128), F32), v((256, LAT), F32),
            v((128, WIDE), BF16), v((4, 64, LAT), BF16),
            pltpu.SMEM((65,), i32), pltpu.SMEM((PAIRS,), i32), pltpu.SMEM((PAIRS,), i32),
            pltpu.SMEM((4,), i32), pltpu.SMEM((4,), i32),
            pltpu.SMEM((1, 64), i32), pltpu.SMEM((128,), i32), pltpu.SMEM((128,), i32),
            dma((16,)), dma((16,)), dma, dma((4,)), dma((16,)), dma((4,)), dma((3,)),
        ],
        compiler_params=pltpu.CompilerParams(vmem_limit_bytes=60 << 20),
        name="attend",
    )(q, kt, latent, lengths, owner, request, kv, blocks)


def local(queries, stream_rows, span_latents, decode_cache, cache_lengths, block_owner, block_request):
    q = queries.reshape(VEC, WIDE)
    stream = stream_rows.reshape(ROWS, WIDE)
    span = span_latents.reshape(ROWS, WIDE)
    owner = block_owner.reshape(128)
    kv, blocks = gather(stream, span, owner)
    out = attend(q, decode_cache.T, stream, cache_lengths, owner, block_request, kv, blocks)
    return out.reshape(1, 1, ROWS, HEADS, LAT)


def solution(mesh):
    return jax.shard_map(
        local,
        mesh=mesh,
        in_specs=(
            P("side", "grp", "seq", None, None),
            P("side", "grp", "seq", None),
            P("grp", "seq", None),
            P(("grp", "seq"), None),
            P(("grp", "seq"), None),
            P(),
            P(),
        ),
        out_specs=P("side", "grp", "seq", None, None),
        check_vma=False,
    )
```

```python
import functools
import math

import jax
import jax.numpy as jnp
from jax import lax
from jax.experimental import pallas as pl
from jax.experimental.pallas import tpu as pltpu
from jax.sharding import PartitionSpec as P

LAT = 512
WIDE = 576
HEADS = 64
ROWS = 64
VEC = ROWS * HEADS
SCALE = 1.4426950408889634 / math.sqrt(192.0)
LOW = -1e30
MESH = pl.DeviceIdType.MESH
F32 = jnp.float32
BF16 = jnp.bfloat16
UNIT = 256
NT = (((1,), (1,)), ((), ()))


def rows(start, size):
    return pl.ds(pl.multiple_of(start, 16), size)


def dot_nt(a, b):
    return lax.dot_general(a, b, NT, preferred_element_type=F32)


def dot_nn(a, b):
    return jnp.dot(a, b, preferred_element_type=F32)


def gather_kernel(
    stream_hbm, span_hbm, owner_hbm, kv_hbm, blk_hbm,
    kv, owner, sendb, recvb, insem, ssem, rsem, dssem, drsem, xssem, xrsem, osem, bsem, wsem,
):
    g = lax.axis_index("grp")
    side = lax.axis_index("side")
    sq = lax.axis_index("seq")
    y, z = sq // 4, sq % 4
    barrier = pltpu.get_barrier_semaphore()

    def device(yy, zz):
        return (yy % 4) * 4 + zz % 4

    @pl.when(side == 0)
    def _():
        for to in [device(y, z + d) for d in (1, 2, 3)] + [device(y + d, z) for d in (1, 2, 3)]:
            pl.semaphore_signal(barrier, inc=1, device_id={"seq": to}, device_id_type=MESH)
        pl.semaphore_signal(barrier, inc=1, device_id={"side": 1}, device_id_type=MESH)

    @pl.when(side == 1)
    def _():
        pl.semaphore_signal(barrier, inc=1, device_id={"side": 0}, device_id_type=MESH)
        for k in range(1, 4):
            pl.semaphore_signal(
                barrier, inc=1, device_id={"grp": (g + k) % 4}, device_id_type=MESH
            )

    def unit_to_decode(u):
        ref = kv.at[rows(u * UNIT, UNIT), :]
        return pltpu.make_async_remote_copy(
            src_ref=ref, dst_ref=ref, send_sem=dssem.at[u], recv_sem=drsem.at[u],
            device_id={"side": 1}, device_id_type=MESH,
        )

    @pl.when(side == 0)
    def _():
        def stream_at(a, b):
            return ((b + 4) % 4) * 256 + ((a + 4) % 4) * 64

        def span_at(a, b):
            return 1024 + ((b + 4) % 4) * 256 + ((a + 4) % 4) * 64

        kinds = (
            (stream_at, z, y, lambda da, db: device(y + db, z + da)),
            (span_at, y, z, lambda da, db: device(y + da, z + db)),
        )
        own = [
            pltpu.make_async_copy(src, kv.at[rows(at(a, b), 64), :], insem.at[n])
            for n, (src, (at, a, b, _)) in enumerate(zip((stream_hbm, span_hbm), kinds))
        ]
        for c in own:
            c.start()
        pl.semaphore_wait(barrier, 7)
        names = {}
        sent = []

        def message(kind, name, start, size, to):
            k = names.setdefault((kind, name), len(names))
            ref = kv.at[rows(start, size), :]
            return pltpu.make_async_remote_copy(
                src_ref=ref, dst_ref=ref, send_sem=ssem.at[k], recv_sem=rsem.at[k],
                device_id={"seq": to}, device_id_type=MESH,
            )

        def send(kind, name, start, size, to):
            c = message(kind, name, start, size, to)
            c.start()
            sent.append(c)

        def take(kind, name, start, size):
            message(kind, name, start, size, sq).wait_recv()

        def both(step):
            for kind in range(2):
                step(kind, *kinds[kind])

        def first(kind, at, a, b, dev):
            own[kind].wait()
            for d in (2, 1, 3):
                send(kind, (0, d), at(a, b), 64, dev(d, 0))
            for d in (2, 1, 3):
                send(kind, (d, 0), at(a, b), 64, dev(0, d))

        def onward(e):
            def step(kind, at, a, b, dev):
                take(kind, (0, e), at(a - e, b), 64)
                for d in (1, 3, 2):
                    send(kind, (d, e), at(a - e, b), 64, dev(0, d))

            return step

        def rest(d):
            def step(kind, at, a, b, dev):
                for e in range(4):
                    take(kind, (d, e), at(a - e, b - d), 64)
                unit_done(kind, (b - d + 4) % 4)

            return step

        def unit_out(u):
            return pltpu.make_async_copy(
                kv.at[rows(u * UNIT, UNIT), :], kv_hbm.at[rows(u * UNIT, UNIT), :], osem.at[u]
            )

        units = []

        def unit_done(kind, u):
            unit_out(u + 4 * kind).start()
            if kind == 0:
                c = unit_to_decode(u)
                c.start()
                units.append(c)

        both(first)
        for e in (1, 3, 2):
            both(onward(e))
        both(lambda kind, at, a, b, dev: unit_done(kind, b))
        for d in (1, 3, 2):
            both(rest(d))
        for u in range(8):
            unit_out(u).wait()
        for c in sent + units:
            c.wait_send()

    @pl.when(side == 1)
    def _():
        names_in = pltpu.make_async_copy(owner_hbm, owner, wsem)
        names_in.start()
        pl.semaphore_wait(barrier, 4)
        names_in.wait()
        lane = lax.broadcasted_iota(jnp.int32, (1, 1024), 1)
        who = [((g + k) % 4) * 16 + sq for k in range(4)]

        def find(b, carry):
            o = owner[g * 32 + b]
            out = []
            for k in range(4):
                n, slots = carry[2 * k], carry[2 * k + 1]
                hit = jnp.where(o == who[k], 1, 0)
                slots = jnp.where(lane // 32 == b, n - (1 - hit) * 8, slots)
                out += [n + hit, slots]
            return tuple(out)

        found = lax.fori_loop(0, 32, find, (jnp.int32(0), jnp.full((1, 1024), -8, jnp.int32)) * 4)
        rowi = lax.broadcasted_iota(jnp.int32, (128, 1024), 0)
        coli = lax.broadcasted_iota(jnp.int32, (128, 1024), 1)
        same = rowi % 32 == coli % 32
        for u in range(4):
            unit_to_decode(u).wait_recv()
        out = []
        for k in (2, 1, 3, 0):
            pick = jnp.where(same & (found[2 * k + 1] == rowi // 32), 1.0, 0.0).astype(BF16)
            sendb[k] = dot_nn(pick, kv[:1024, :]).astype(BF16)
            if k:
                c = pltpu.make_async_remote_copy(
                    src_ref=sendb.at[k], dst_ref=recvb.at[g], send_sem=xssem.at[k],
                    recv_sem=xrsem.at[g], device_id={"grp": (g + k) % 4}, device_id_type=MESH,
                )
            else:
                c = pltpu.make_async_copy(sendb.at[0], blk_hbm.at[g], bsem.at[0])
            c.start()
            out.append(c)
        for k in range(1, 4):
            h = (g + k) % 4
            pltpu.make_async_remote_copy(
                src_ref=sendb.at[k], dst_ref=recvb.at[h], send_sem=xssem.at[k], recv_sem=xrsem.at[h],
                device_id={"grp": h}, device_id_type=MESH,
            ).wait_recv()
            c = pltpu.make_async_copy(recvb.at[h], blk_hbm.at[h], bsem.at[k])
            c.start()
            out.append(c)
        for n, c in enumerate(out):
            if n < 3:
                c.wait_send()
            else:
                c.wait()


def gather(stream, span, owner):
    hbm = pl.BlockSpec(memory_space=pltpu.HBM)
    v = pltpu.VMEM
    dma = pltpu.SemaphoreType.DMA
    return pl.pallas_call(
        gather_kernel,
        out_shape=(
            jax.ShapeDtypeStruct((2048, WIDE), BF16),
            jax.ShapeDtypeStruct((4, 128, WIDE), BF16),
        ),
        in_specs=[hbm, hbm, hbm],
        out_specs=(hbm, hbm),
        scratch_shapes=[
            v((2048, WIDE), BF16), pltpu.SMEM((128,), jnp.int32),
            v((4, 128, WIDE), BF16), v((4, 128, WIDE), BF16),
            dma((2,)), dma((40,)), dma((40,)), dma((4,)), dma((4,)), dma((4,)), dma((4,)), dma((8,)),
            dma((4,)), dma,
        ],
        compiler_params=pltpu.CompilerParams(
            vmem_limit_bytes=60 << 20, collective_id=0, has_side_effects=True
        ),
        name="gather_latents",
    )(stream, span, owner)


PAIRS = 32
BQ = 256
WIN = 384


def prefill_side(q_hbm, kv_hbm, out_hbm, qv, kv, ov, bias, s0, s1, p0, p1, l0, l1, qsem, ksem, osem):
    sq = lax.axis_index("seq")
    nb = VEC // BQ

    def q_copy(i):
        r = rows(i * BQ, BQ)
        return pltpu.make_async_copy(q_hbm.at[r, :], qv.at[r, :], qsem.at[i])

    def k_copy(u):
        r = rows(u * 512, 512)
        return pltpu.make_async_copy(kv_hbm.at[r, :], kv.at[r, :], ksem.at[u])

    q_copy(0).start()
    for u in range(4):
        k_copy(u).start()
    for i in range(1, nb):
        q_copy(i).start()
    row = sq * 64 + lax.broadcasted_iota(jnp.int32, (64, 1024), 0)
    j = lax.broadcasted_iota(jnp.int32, (64, 1024), 1)
    pos = (((j // 64) % 4) * 4 + j // 256) * 64 + j % 64
    bias[...] = jnp.where(pos <= row, 0.0, LOW)

    parts = 4
    kc, rc = 2048 // parts, BQ // parts

    def scores(i, s, c):
        keys = slice(kc * c, kc * c + kc)
        s[:, keys] = dot_nt(qv[rows(i * BQ, BQ), :], kv[keys, :])

    def soft(i, s, pr, l, c):
        r = slice(rc * c, rc * c + rc)
        xa = s[r, :1024]
        xb = s[r, 1024:] + bias[pl.ds(i * 4 + (rc * c) // 64, 1), :]
        m = jnp.maximum(jnp.max(xa, axis=1, keepdims=True), jnp.max(xb, axis=1, keepdims=True)) * SCALE
        ea = jnp.exp2(xa * SCALE - m)
        eb = jnp.exp2(xb * SCALE - m)
        pr[r, :1024] = ea.astype(BF16)
        pr[r, 1024:] = eb.astype(BF16)
        t = jnp.sum(ea, axis=1, keepdims=True) + jnp.sum(eb, axis=1, keepdims=True)
        l[r, :] = jnp.broadcast_to(t, (rc, 128))

    def out_copy(i):
        r = rows(i * BQ, 2 * BQ)
        return pltpu.make_async_copy(ov.at[r, :], out_hbm.at[r, :], osem.at[i // 2])

    def values(i, pr, l, h):
        cols = slice(256 * h, 256 * h + 256)
        a = dot_nn(pr[...], kv[:, cols])
        ov[rows(i * BQ, BQ), cols] = (a * (1.0 / l[:, :1])).astype(BF16)

    q_copy(0).wait()
    for c in range(parts):
        k_copy(c).wait()
        scores(0, s0, c)
    q_copy(1).wait()
    for c in range(parts):
        scores(1, s1, c)
        soft(0, s0, p0, l0, c)

    def half(i, sa, sb, pa, pb, la, lb):
        for c in range(parts):
            scores(i + 2, sa, c)
            soft(i + 1, sb, pb, lb, c)
            if c == parts // 2 - 1:
                values(i, pa, la, 0)
        values(i, pa, la, 1)

    def body(t, _):
        i = 2 * t
        q_copy(i + 2).wait()
        q_copy(i + 3).wait()
        half(i, s0, s1, p0, p1, l0, l1)
        half(i + 1, s1, s0, p1, p0, l1, l0)
        out_copy(i).start()
        return 0

    lax.fori_loop(0, nb // 2 - 1, body, 0)
    for c in range(parts):
        soft(nb - 1, s1, p1, l1, c)
    for h in range(2):
        values(nb - 2, p0, l0, h)
    for h in range(2):
        values(nb - 1, p1, l1, h)
    out_copy(nb - 2).start()
    for t in range(nb // 2):
        out_copy(2 * t).wait()


def decode_side(
    q_hbm, kt_hbm, lat_hbm, blk_hbm, len_ref, owner, request, out_hbm,
    qv, kt, lat, latf, ov, selfs, s0, s1, p0, p1, m0, m1, l0, l1, mrun, lrun, acc, arr, ob,
    starts, pc, pt, req, src, qsem, ksem, lsem, asem, osem, fsem,
):
    me = lax.axis_index("grp") * 16 + lax.axis_index("seq")

    def q_copy(c):
        r = rows(c * 256, 256)
        return pltpu.make_async_copy(q_hbm.at[r, :], qv.at[r, :], qsem.at[c])

    def k_copy(t):
        r = pl.ds(pl.multiple_of(t * 256, 256), 256)
        return pltpu.make_async_copy(kt_hbm.at[:, r], kt.at[:, r], ksem.at[t])

    def o_copy(c):
        r = rows(c * 256, 256)
        return pltpu.make_async_copy(ov.at[r, :], out_hbm.at[r, :], osem.at[c])

    lat_copy = pltpu.make_async_copy(lat_hbm, lat, lsem)
    lat_copy.start()
    for c in range(16):
        q_copy(c).start()
    for t in range(16):
        k_copy(t).start()

    def scan(r, total):
        starts[r] = total
        return total + len_ref[0, r]

    starts[64] = lax.fori_loop(0, 64, scan, jnp.int32(0))

    def fill(p, carry):
        c, t = carry
        pc[p] = jnp.minimum(c, 15)
        pt[p] = jnp.where(c < 16, t, -1)
        cc = jnp.minimum(c, 15)
        more = (t + 1) * UNIT < starts[cc * 4 + 4]
        nc = jnp.where(more, c, c + 1)
        ns = starts[jnp.minimum(nc, 15) * 4]
        nt = jnp.where(more, t + 1, ns // UNIT)
        return nc, nt

    lax.fori_loop(0, PAIRS, fill, (jnp.int32(0), jnp.int32(0)))
    for i in range(4):
        req[i] = 0
        src[i] = 0

    def find(b, carry):
        n, rank = carry
        rank = jnp.where(b % 32 == 0, 0, rank)
        hit = owner[b] == me

        @pl.when(hit)
        def _():
            req[n] = request[b]
            src[n] = (b // 32) * 4 + rank

        h = hit.astype(jnp.int32)
        return n + h, rank + h

    n, _ = lax.fori_loop(0, 128, find, (jnp.int32(0), jnp.int32(0)))
    arrivals = []
    for i in range(4):
        s = src[i]
        arrivals.append(
            pltpu.make_async_copy(
                blk_hbm.at[s // 4, pl.ds(pl.multiple_of((s % 4) * 32, 32), 32), :],
                arr.at[pl.ds(32 * i, 32), :], asem.at[i],
            )
        )
    for c in arrivals:
        c.start()
    lat_copy.wait()
    latf[...] = lat[...].astype(F32)

    def own(c, _):
        q_copy(c).wait()
        for k in range(4):
            r = c * 4 + k
            rr = pl.ds(pl.multiple_of(r * 64, 64), 64)
            d = jnp.sum(qv[rr, :].astype(F32) * latf[pl.ds(r, 1), :], axis=1, keepdims=True)
            selfs[rr, :] = jnp.broadcast_to(d, (64, 128))
        return 0

    lax.fori_loop(0, 16, own, 0)
    for t in range(16):
        k_copy(t).wait()

    def cols(p):
        t = jnp.maximum(pt[p], 0)
        return pl.ds(pl.multiple_of(t * UNIT, UNIT), UNIT)

    def crows(p):
        return pl.ds(pl.multiple_of(pc[p] * 256, 256), 256)

    def qk(p, s):
        s[...] = dot_nn(qv[crows(p), :], kt[:, cols(p)])

    def soft(p, s, pr, m, l):
        c, t = pc[p], pt[p]
        base = t * UNIT
        col = lax.broadcasted_iota(jnp.int32, (64, UNIT), 1)
        for k in range(4):
            rr = slice(64 * k, 64 * k + 64)
            lo = jnp.where(t < 0, 1 << 20, starts[c * 4 + k] - base)
            hi = starts[c * 4 + k + 1] - base
            x = jnp.where((col >= lo) & (col < hi), s[rr, :], LOW)
            mx = jnp.max(x, axis=1, keepdims=True)
            e = jnp.exp2((x - mx) * SCALE)
            m[rr, :] = jnp.broadcast_to(mx, (64, 128))
            l[rr, :] = jnp.broadcast_to(jnp.sum(e, axis=1, keepdims=True), (64, 128))
            pr[rr, :] = e.astype(BF16)

    def pv(p, pr, m, l):
        c = pc[p]
        new = (p == 0) | (pc[jnp.maximum(p - 1, 0)] != c)
        o = dot_nt(pr[...], kt[:LAT, cols(p)])
        for k in range(4):
            rr = slice(64 * k, 64 * k + 64)
            r = c * 4 + k
            g = pl.ds(pl.multiple_of(r * 64, 64), 64)
            mo = jnp.where(new, selfs[g, :], mrun[rr, :])
            lo = jnp.where(new, 1.0, lrun[rr, :])
            ao = jnp.where(new, jnp.broadcast_to(latf[pl.ds(r, 1), :LAT], (64, LAT)), acc[rr, :])
            mn = jnp.maximum(mo, m[rr, :])
            al = jnp.exp2((mo - mn) * SCALE)
            be = jnp.exp2((m[rr, :] - mn) * SCALE)
            ln = lo * al + l[rr, :] * be
            an = ao * al[:, :1] + o[rr, :] * be[:, :1]
            mrun[rr, :] = mn
            lrun[rr, :] = ln
            acc[rr, :] = an
            ov[g, :] = (an * (1.0 / ln[:, :1])).astype(BF16)

    qk(0, s0)
    qk(1, s1)
    soft(0, s0, p0, m0, l0)

    def send(c, _):
        o_copy(c).start()
        return 0

    def body(i, done):
        j = 2 * i
        qk(j + 2, s0)
        soft(j + 1, s1, p1, m1, l1)
        pv(j, p0, m0, l0)
        qk(j + 3, s1)
        soft(j + 2, s0, p0, m0, l0)
        pv(j + 1, p1, m1, l1)
        now = pc[j + 2]
        lax.fori_loop(done, now, send, 0)
        return now

    done = lax.fori_loop(0, PAIRS // 2 - 1, body, jnp.int32(0))
    soft(PAIRS - 1, s1, p1, m1, l1)
    pv(PAIRS - 2, p0, m0, l0)
    pv(PAIRS - 1, p1, m1, l1)
    lax.fori_loop(done, 16, send, 0)

    for c in arrivals:
        c.wait()
    writes = []
    for i in range(4):
        ok = i < n
        for j in range(i):
            ok = ok & (req[j] != req[i])
        writes.append(ok)

        @pl.when(ok)
        def _(i=i):
            r = req[i]
            w = jnp.minimum(starts[r] // 128, (4096 - WIN) // 128) * 128
            win = pl.ds(pl.multiple_of(w, 128), WIN)
            rr = pl.ds(pl.multiple_of(r * 64, 64), 64)
            q = qv[rr, :]
            x3 = selfs[rr, :][:, :1]
            x1 = dot_nn(q, kt[:, win])
            col = lax.broadcasted_iota(jnp.int32, (64, WIN), 1) + w
            x1 = jnp.where((col >= starts[r]) & (col < starts[r + 1]), x1, LOW)
            x2 = dot_nt(q, arr[...])
            slot = lax.broadcasted_iota(jnp.int32, (64, 128), 1) // 32
            seen = (slot == 0) & ((0 < n) & (req[0] == r))
            for j in range(1, 4):
                seen = seen | ((slot == j) & ((j < n) & (req[j] == r)))
            x2 = jnp.where(seen, x2, LOW)
            m = jnp.maximum(
                x3,
                jnp.maximum(jnp.max(x1, axis=1, keepdims=True), jnp.max(x2, axis=1, keepdims=True)),
            )
            e1 = jnp.exp2((x1 - m) * SCALE)
            e2 = jnp.exp2((x2 - m) * SCALE)
            e3 = jnp.exp2((x3 - m) * SCALE)
            l = jnp.sum(e1, axis=1, keepdims=True) + jnp.sum(e2, axis=1, keepdims=True) + e3
            o = dot_nt(e1.astype(BF16), kt[:LAT, win]) + dot_nn(e2.astype(BF16), arr[:, :LAT])
            o = o + e3 * latf[pl.ds(r, 1), :LAT]
            ob[i] = (o * (1.0 / l)).astype(BF16)

    for c in range(16):
        o_copy(c).wait()

    def fix_copy(i):
        return pltpu.make_async_copy(
            ob.at[i], out_hbm.at[pl.ds(pl.multiple_of(req[i] * 64, 64), 64), :], fsem.at[i]
        )

    for i in range(4):
        @pl.when(writes[i])
        def _(i=i):
            fix_copy(i).start()

    for i in range(4):
        @pl.when(writes[i])
        def _(i=i):
            fix_copy(i).wait()


def attend_kernel(
    q_hbm, kt_hbm, lat_hbm, len_hbm, owner_hbm, request_hbm, kv_hbm, blk_hbm, out_hbm,
    qv, kv, bias, ps0, ps1, pp0, pp1, pl0, pl1,
    kt, lat, latf, ov, selfs, s0, s1, p0, p1, m0, m1, l0, l1, mrun, lrun, acc, arr, ob,
    starts, pc, pt, req, src, len_ref, owner, request, qsem, ksem, lsem, asem, osem, fsem, isem,
):
    side = lax.axis_index("side")

    @pl.when(side == 0)
    def _():
        prefill_side(
            q_hbm, kv_hbm, out_hbm, qv, kv, ov, bias, ps0, ps1, pp0, pp1, pl0, pl1, qsem, ksem, osem
        )

    @pl.when(side == 1)
    def _():
        small = [
            pltpu.make_async_copy(a, b, isem.at[n])
            for n, (a, b) in enumerate(
                ((len_hbm, len_ref), (owner_hbm, owner), (request_hbm, request))
            )
        ]
        for c in small:
            c.start()
        for c in small:
            c.wait()
        decode_side(
            q_hbm, kt_hbm, lat_hbm, blk_hbm, len_ref, owner, request, out_hbm,
            qv, kt, lat, latf, ov, selfs, s0, s1, p0, p1, m0, m1, l0, l1, mrun, lrun, acc, arr, ob,
            starts, pc, pt, req, src, qsem, ksem, lsem, asem, osem, fsem,
        )


def attend(q, kt, latent, lengths, owner, request, kv, blocks):
    any_ = pl.BlockSpec(memory_space=pltpu.HBM)
    v = pltpu.VMEM
    i32 = jnp.int32
    dma = pltpu.SemaphoreType.DMA
    return pl.pallas_call(
        attend_kernel,
        out_shape=jax.ShapeDtypeStruct((VEC, LAT), BF16),
        in_specs=[any_] * 8,
        out_specs=any_,
        scratch_shapes=[
            v((VEC, WIDE), BF16), v((2048, WIDE), BF16), v((64, 1024), F32),
            v((BQ, 2048), F32), v((BQ, 2048), F32), v((BQ, 2048), BF16), v((BQ, 2048), BF16),
            v((BQ, 128), F32), v((BQ, 128), F32),
            v((WIDE, 4096), BF16), v((64, WIDE), BF16), v((64, WIDE), F32), v((VEC, LAT), BF16),
            v((VEC, 128), F32),
            v((256, UNIT), F32), v((256, UNIT), F32), v((256, UNIT), BF16), v((256, UNIT), BF16),
            v((256, 128), F32), v((256, 128), F32), v((256, 128), F32), v((256, 128), F32),
            v((256, 128), F32), v((256, 128), F32), v((256, LAT), F32),
            v((128, WIDE), BF16), v((4, 64, LAT), BF16),
            pltpu.SMEM((65,), i32), pltpu.SMEM((PAIRS,), i32), pltpu.SMEM((PAIRS,), i32),
            pltpu.SMEM((4,), i32), pltpu.SMEM((4,), i32),
            pltpu.SMEM((1, 64), i32), pltpu.SMEM((128,), i32), pltpu.SMEM((128,), i32),
            dma((16,)), dma((16,)), dma, dma((4,)), dma((16,)), dma((4,)), dma((3,)),
        ],
        compiler_params=pltpu.CompilerParams(vmem_limit_bytes=60 << 20),
        name="attend",
    )(q, kt, latent, lengths, owner, request, kv, blocks)


def local(queries, stream_rows, span_latents, decode_cache, cache_lengths, block_owner, block_request):
    q = queries.reshape(VEC, WIDE)
    stream = stream_rows.reshape(ROWS, WIDE)
    span = span_latents.reshape(ROWS, WIDE)
    owner = block_owner.reshape(128)
    kv, blocks = gather(stream, span, owner)
    out = attend(q, decode_cache.T, stream, cache_lengths, owner, block_request, kv, blocks)
    return out.reshape(1, 1, ROWS, HEADS, LAT)


def solution(mesh):
    return jax.shard_map(
        local,
        mesh=mesh,
        in_specs=(
            P("side", "grp", "seq", None, None),
            P("side", "grp", "seq", None),
            P("grp", "seq", None),
            P(("grp", "seq"), None),
            P(("grp", "seq"), None),
            P(),
            P(),
        ),
        out_specs=P("side", "grp", "seq", None, None),
        check_vma=False,
    )
```

```python
import functools
import math

import jax
import jax.numpy as jnp
from jax import lax
from jax.experimental import pallas as pl
from jax.experimental.pallas import tpu as pltpu
from jax.sharding import PartitionSpec as P

LAT = 512
WIDE = 576
HEADS = 64
ROWS = 64
VEC = ROWS * HEADS
SCALE = 1.4426950408889634 / math.sqrt(192.0)
LOW = -1e30
MESH = pl.DeviceIdType.MESH
F32 = jnp.float32
BF16 = jnp.bfloat16
UNIT = 256
NT = (((1,), (1,)), ((), ()))


def rows(start, size):
    return pl.ds(pl.multiple_of(start, 16), size)


def dot_nt(a, b):
    return lax.dot_general(a, b, NT, preferred_element_type=F32)


def dot_nn(a, b):
    return jnp.dot(a, b, preferred_element_type=F32)


def gather_kernel(
    stream_hbm, span_hbm, owner_hbm, kv_hbm, blk_hbm,
    kv, owner, sendb, recvb, insem, ssem, rsem, dssem, drsem, xssem, xrsem, osem, bsem, wsem,
):
    g = lax.axis_index("grp")
    side = lax.axis_index("side")
    sq = lax.axis_index("seq")
    y, z = sq // 4, sq % 4
    barrier = pltpu.get_barrier_semaphore()

    def device(yy, zz):
        return (yy % 4) * 4 + zz % 4

    @pl.when(side == 0)
    def _():
        for to in [device(y, z + d) for d in (1, 2, 3)] + [device(y + d, z) for d in (1, 2, 3)]:
            pl.semaphore_signal(barrier, inc=1, device_id={"seq": to}, device_id_type=MESH)
        pl.semaphore_signal(barrier, inc=1, device_id={"side": 1}, device_id_type=MESH)

    @pl.when(side == 1)
    def _():
        pl.semaphore_signal(barrier, inc=1, device_id={"side": 0}, device_id_type=MESH)
        for k in range(1, 4):
            pl.semaphore_signal(
                barrier, inc=1, device_id={"grp": (g + k) % 4}, device_id_type=MESH
            )

    def unit_to_decode(u):
        ref = kv.at[rows(u * UNIT, UNIT), :]
        return pltpu.make_async_remote_copy(
            src_ref=ref, dst_ref=ref, send_sem=dssem.at[u], recv_sem=drsem.at[u],
            device_id={"side": 1}, device_id_type=MESH,
        )

    @pl.when(side == 0)
    def _():
        def stream_at(a, b):
            return ((b + 4) % 4) * 256 + ((a + 4) % 4) * 64

        def span_at(a, b):
            return 1024 + ((b + 4) % 4) * 256 + ((a + 4) % 4) * 64

        kinds = (
            (stream_at, z, y, lambda da, db: device(y + db, z + da)),
            (span_at, y, z, lambda da, db: device(y + da, z + db)),
        )
        own = [
            pltpu.make_async_copy(src, kv.at[rows(at(a, b), 64), :], insem.at[n])
            for n, (src, (at, a, b, _)) in enumerate(zip((stream_hbm, span_hbm), kinds))
        ]
        for c in own:
            c.start()
        pl.semaphore_wait(barrier, 7)
        names = {}
        sent = []

        def message(kind, name, start, size, to):
            k = names.setdefault((kind, name), len(names))
            ref = kv.at[rows(start, size), :]
            return pltpu.make_async_remote_copy(
                src_ref=ref, dst_ref=ref, send_sem=ssem.at[k], recv_sem=rsem.at[k],
                device_id={"seq": to}, device_id_type=MESH,
            )

        def send(kind, name, start, size, to):
            c = message(kind, name, start, size, to)
            c.start()
            sent.append(c)

        def take(kind, name, start, size):
            message(kind, name, start, size, sq).wait_recv()

        def both(step):
            for kind in range(2):
                step(kind, *kinds[kind])

        def first(kind, at, a, b, dev):
            own[kind].wait()
            for d in (2, 1, 3):
                send(kind, (0, d), at(a, b), 64, dev(d, 0))
            for d in (2, 1, 3):
                send(kind, (d, 0), at(a, b), 64, dev(0, d))

        def onward(e):
            def step(kind, at, a, b, dev):
                take(kind, (0, e), at(a - e, b), 64)
                for d in (1, 3, 2):
                    send(kind, (d, e), at(a - e, b), 64, dev(0, d))

            return step

        def rest(d):
            def step(kind, at, a, b, dev):
                for e in range(4):
                    take(kind, (d, e), at(a - e, b - d), 64)
                unit_done(kind, (b - d + 4) % 4)

            return step

        def unit_out(u):
            return pltpu.make_async_copy(
                kv.at[rows(u * UNIT, UNIT), :], kv_hbm.at[rows(u * UNIT, UNIT), :], osem.at[u]
            )

        units = []

        def unit_done(kind, u):
            unit_out(u + 4 * kind).start()
            if kind == 0:
                c = unit_to_decode(u)
                c.start()
                units.append(c)

        both(first)
        for e in (1, 3, 2):
            both(onward(e))
        both(lambda kind, at, a, b, dev: unit_done(kind, b))
        for d in (1, 3, 2):
            both(rest(d))
        for u in range(8):
            unit_out(u).wait()
        for c in sent + units:
            c.wait_send()

    @pl.when(side == 1)
    def _():
        names_in = pltpu.make_async_copy(owner_hbm, owner, wsem)
        names_in.start()
        pl.semaphore_wait(barrier, 4)
        names_in.wait()
        lane = lax.broadcasted_iota(jnp.int32, (1, 1024), 1)
        who = [((g + k) % 4) * 16 + sq for k in range(4)]

        def find(b, carry):
            o = owner[g * 32 + b]
            out = []
            for k in range(4):
                n, slots = carry[2 * k], carry[2 * k + 1]
                hit = jnp.where(o == who[k], 1, 0)
                slots = jnp.where(lane // 32 == b, n - (1 - hit) * 8, slots)
                out += [n + hit, slots]
            return tuple(out)

        found = lax.fori_loop(0, 32, find, (jnp.int32(0), jnp.full((1, 1024), -8, jnp.int32)) * 4)
        rowi = lax.broadcasted_iota(jnp.int32, (128, 1024), 0)
        coli = lax.broadcasted_iota(jnp.int32, (128, 1024), 1)
        same = rowi % 32 == coli % 32
        for u in range(4):
            unit_to_decode(u).wait_recv()
        out = []
        for k in (2, 1, 3, 0):
            pick = jnp.where(same & (found[2 * k + 1] == rowi // 32), 1.0, 0.0).astype(BF16)
            sendb[k] = dot_nn(pick, kv[:1024, :]).astype(BF16)
            if k:
                c = pltpu.make_async_remote_copy(
                    src_ref=sendb.at[k], dst_ref=recvb.at[g], send_sem=xssem.at[k],
                    recv_sem=xrsem.at[g], device_id={"grp": (g + k) % 4}, device_id_type=MESH,
                )
            else:
                c = pltpu.make_async_copy(sendb.at[0], blk_hbm.at[g], bsem.at[0])
            c.start()
            out.append(c)
        for k in range(1, 4):
            h = (g + k) % 4
            pltpu.make_async_remote_copy(
                src_ref=sendb.at[k], dst_ref=recvb.at[h], send_sem=xssem.at[k], recv_sem=xrsem.at[h],
                device_id={"grp": h}, device_id_type=MESH,
            ).wait_recv()
            c = pltpu.make_async_copy(recvb.at[h], blk_hbm.at[h], bsem.at[k])
            c.start()
            out.append(c)
        for n, c in enumerate(out):
            if n < 3:
                c.wait_send()
            else:
                c.wait()


def gather(stream, span, owner):
    hbm = pl.BlockSpec(memory_space=pltpu.HBM)
    v = pltpu.VMEM
    dma = pltpu.SemaphoreType.DMA
    return pl.pallas_call(
        gather_kernel,
        out_shape=(
            jax.ShapeDtypeStruct((2048, WIDE), BF16),
            jax.ShapeDtypeStruct((4, 128, WIDE), BF16),
        ),
        in_specs=[hbm, hbm, hbm],
        out_specs=(hbm, hbm),
        scratch_shapes=[
            v((2048, WIDE), BF16), pltpu.SMEM((128,), jnp.int32),
            v((4, 128, WIDE), BF16), v((4, 128, WIDE), BF16),
            dma((2,)), dma((40,)), dma((40,)), dma((4,)), dma((4,)), dma((4,)), dma((4,)), dma((8,)),
            dma((4,)), dma,
        ],
        compiler_params=pltpu.CompilerParams(
            vmem_limit_bytes=60 << 20, collective_id=0, has_side_effects=True
        ),
        name="gather_latents",
    )(stream, span, owner)


PAIRS = 32
BQ = 256
WIN = 384


def prefill_side(q_hbm, kv_hbm, out_hbm, qv, kv, ov, bias, s0, s1, p0, p1, l0, l1, qsem, ksem, osem):
    sq = lax.axis_index("seq")
    nb = VEC // BQ

    def q_copy(i):
        r = rows(i * BQ, BQ)
        return pltpu.make_async_copy(q_hbm.at[r, :], qv.at[r, :], qsem.at[i])

    def k_copy(u):
        r = rows(u * 512, 512)
        return pltpu.make_async_copy(kv_hbm.at[r, :], kv.at[r, :], ksem.at[u])

    q_copy(0).start()
    for u in range(4):
        k_copy(u).start()
    for i in range(1, 4):
        q_copy(i).start()
    row = sq * 64 + lax.broadcasted_iota(jnp.int32, (64, 1024), 0)
    j = lax.broadcasted_iota(jnp.int32, (64, 1024), 1)
    pos = (((j // 64) % 4) * 4 + j // 256) * 64 + j % 64
    bias[...] = jnp.where(pos <= row, 0.0, LOW)

    parts = 4
    kc, rc = 2048 // parts, BQ // parts

    def scores(i, s, c):
        keys = slice(kc * c, kc * c + kc)
        s[:, keys] = dot_nt(qv[rows(i * BQ, BQ), :], kv[keys, :])

    def soft(i, s, pr, l, c):
        r = slice(rc * c, rc * c + rc)
        xa = s[r, :1024]
        xb = s[r, 1024:] + bias[pl.ds(i * 4 + (rc * c) // 64, 1), :]
        m = jnp.maximum(jnp.max(xa, axis=1, keepdims=True), jnp.max(xb, axis=1, keepdims=True)) * SCALE
        ea = jnp.exp2(xa * SCALE - m)
        eb = jnp.exp2(xb * SCALE - m)
        pr[r, :1024] = ea.astype(BF16)
        pr[r, 1024:] = eb.astype(BF16)
        t = jnp.sum(ea, axis=1, keepdims=True) + jnp.sum(eb, axis=1, keepdims=True)
        l[r, :] = jnp.broadcast_to(t, (rc, 128))

    def out_copy(i):
        r = rows(i * BQ, 2 * BQ)
        return pltpu.make_async_copy(ov.at[r, :], out_hbm.at[r, :], osem.at[i // 2])

    def values(i, pr, l, h):
        cols = slice(256 * h, 256 * h + 256)
        a = dot_nn(pr[...], kv[:, cols])
        ov[rows(i * BQ, BQ), cols] = (a * (1.0 / l[:, :1])).astype(BF16)

    q_copy(0).wait()
    for c in range(parts):
        k_copy(c).wait()
        if c == parts - 1:
            for i in range(4, nb):
                q_copy(i).start()
        scores(0, s0, c)
    q_copy(1).wait()
    for c in range(parts):
        scores(1, s1, c)
        soft(0, s0, p0, l0, c)

    def half(i, sa, sb, pa, pb, la, lb):
        for c in range(parts):
            scores(i + 2, sa, c)
            soft(i + 1, sb, pb, lb, c)
            if c == parts // 2 - 1:
                values(i, pa, la, 0)
        values(i, pa, la, 1)

    def body(t, _):
        i = 2 * t
        q_copy(i + 2).wait()
        q_copy(i + 3).wait()
        half(i, s0, s1, p0, p1, l0, l1)
        half(i + 1, s1, s0, p1, p0, l1, l0)
        out_copy(i).start()
        return 0

    lax.fori_loop(0, nb // 2 - 1, body, 0)
    for c in range(parts):
        soft(nb - 1, s1, p1, l1, c)
    for h in range(2):
        values(nb - 2, p0, l0, h)
    for h in range(2):
        values(nb - 1, p1, l1, h)
    out_copy(nb - 2).start()
    for t in range(nb // 2):
        out_copy(2 * t).wait()


def decode_side(
    q_hbm, kt_hbm, lat_hbm, blk_hbm, len_ref, owner, request, out_hbm,
    qv, kt, lat, latf, ov, selfs, s0, s1, p0, p1, m0, m1, l0, l1, mrun, lrun, acc, arr, ob,
    starts, pc, pt, req, src, qsem, ksem, lsem, asem, osem, fsem,
):
    me = lax.axis_index("grp") * 16 + lax.axis_index("seq")

    def q_copy(c):
        r = rows(c * 256, 256)
        return pltpu.make_async_copy(q_hbm.at[r, :], qv.at[r, :], qsem.at[c])

    def k_copy(t):
        r = pl.ds(pl.multiple_of(t * 256, 256), 256)
        return pltpu.make_async_copy(kt_hbm.at[:, r], kt.at[:, r], ksem.at[t])

    def o_copy(c):
        r = rows(c * 256, 256)
        return pltpu.make_async_copy(ov.at[r, :], out_hbm.at[r, :], osem.at[c])

    lat_copy = pltpu.make_async_copy(lat_hbm, lat, lsem)
    lat_copy.start()
    for c in range(16):
        q_copy(c).start()
    for t in range(16):
        k_copy(t).start()

    def scan(r, total):
        starts[r] = total
        return total + len_ref[0, r]

    starts[64] = lax.fori_loop(0, 64, scan, jnp.int32(0))

    def fill(p, carry):
        c, t = carry
        pc[p] = jnp.minimum(c, 15)
        pt[p] = jnp.where(c < 16, t, -1)
        cc = jnp.minimum(c, 15)
        more = (t + 1) * UNIT < starts[cc * 4 + 4]
        nc = jnp.where(more, c, c + 1)
        ns = starts[jnp.minimum(nc, 15) * 4]
        nt = jnp.where(more, t + 1, ns // UNIT)
        return nc, nt

    lax.fori_loop(0, PAIRS, fill, (jnp.int32(0), jnp.int32(0)))
    for i in range(4):
        req[i] = 0
        src[i] = 0

    def find(b, carry):
        n, rank = carry
        rank = jnp.where(b % 32 == 0, 0, rank)
        hit = owner[b] == me

        @pl.when(hit)
        def _():
            req[n] = request[b]
            src[n] = (b // 32) * 4 + rank

        h = hit.astype(jnp.int32)
        return n + h, rank + h

    n, _ = lax.fori_loop(0, 128, find, (jnp.int32(0), jnp.int32(0)))
    arrivals = []
    for i in range(4):
        s = src[i]
        arrivals.append(
            pltpu.make_async_copy(
                blk_hbm.at[s // 4, pl.ds(pl.multiple_of((s % 4) * 32, 32), 32), :],
                arr.at[pl.ds(32 * i, 32), :], asem.at[i],
            )
        )
    for c in arrivals:
        c.start()
    lat_copy.wait()
    latf[...] = lat[...].astype(F32)

    def own(c, _):
        q_copy(c).wait()
        for k in range(4):
            r = c * 4 + k
            rr = pl.ds(pl.multiple_of(r * 64, 64), 64)
            d = jnp.sum(qv[rr, :].astype(F32) * latf[pl.ds(r, 1), :], axis=1, keepdims=True)
            selfs[rr, :] = jnp.broadcast_to(d, (64, 128))
        return 0

    lax.fori_loop(0, 16, own, 0)
    for t in range(16):
        k_copy(t).wait()

    def cols(p):
        t = jnp.maximum(pt[p], 0)
        return pl.ds(pl.multiple_of(t * UNIT, UNIT), UNIT)

    def crows(p):
        return pl.ds(pl.multiple_of(pc[p] * 256, 256), 256)

    def qk(p, s):
        s[...] = dot_nn(qv[crows(p), :], kt[:, cols(p)])

    def soft(p, s, pr, m, l):
        c, t = pc[p], pt[p]
        base = t * UNIT
        col = lax.broadcasted_iota(jnp.int32, (64, UNIT), 1)
        for k in range(4):
            rr = slice(64 * k, 64 * k + 64)
            lo = jnp.where(t < 0, 1 << 20, starts[c * 4 + k] - base)
            hi = starts[c * 4 + k + 1] - base
            x = jnp.where((col >= lo) & (col < hi), s[rr, :], LOW)
            mx = jnp.max(x, axis=1, keepdims=True)
            e = jnp.exp2((x - mx) * SCALE)
            m[rr, :] = jnp.broadcast_to(mx, (64, 128))
            l[rr, :] = jnp.broadcast_to(jnp.sum(e, axis=1, keepdims=True), (64, 128))
            pr[rr, :] = e.astype(BF16)

    def pv(p, pr, m, l):
        c = pc[p]
        new = (p == 0) | (pc[jnp.maximum(p - 1, 0)] != c)
        o = dot_nt(pr[...], kt[:LAT, cols(p)])
        for k in range(4):
            rr = slice(64 * k, 64 * k + 64)
            r = c * 4 + k
            g = pl.ds(pl.multiple_of(r * 64, 64), 64)
            mo = jnp.where(new, selfs[g, :], mrun[rr, :])
            lo = jnp.where(new, 1.0, lrun[rr, :])
            ao = jnp.where(new, jnp.broadcast_to(latf[pl.ds(r, 1), :LAT], (64, LAT)), acc[rr, :])
            mn = jnp.maximum(mo, m[rr, :])
            al = jnp.exp2((mo - mn) * SCALE)
            be = jnp.exp2((m[rr, :] - mn) * SCALE)
            ln = lo * al + l[rr, :] * be
            an = ao * al[:, :1] + o[rr, :] * be[:, :1]
            mrun[rr, :] = mn
            lrun[rr, :] = ln
            acc[rr, :] = an
            ov[g, :] = (an * (1.0 / ln[:, :1])).astype(BF16)

    qk(0, s0)
    qk(1, s1)
    soft(0, s0, p0, m0, l0)

    def send(c, _):
        o_copy(c).start()
        return 0

    def body(i, done):
        j = 2 * i
        qk(j + 2, s0)
        soft(j + 1, s1, p1, m1, l1)
        pv(j, p0, m0, l0)
        qk(j + 3, s1)
        soft(j + 2, s0, p0, m0, l0)
        pv(j + 1, p1, m1, l1)
        now = pc[j + 2]
        lax.fori_loop(done, now, send, 0)
        return now

    done = lax.fori_loop(0, PAIRS // 2 - 1, body, jnp.int32(0))
    soft(PAIRS - 1, s1, p1, m1, l1)
    pv(PAIRS - 2, p0, m0, l0)
    pv(PAIRS - 1, p1, m1, l1)
    lax.fori_loop(done, 16, send, 0)

    for c in arrivals:
        c.wait()
    writes = []
    for i in range(4):
        ok = i < n
        for j in range(i):
            ok = ok & (req[j] != req[i])
        writes.append(ok)

        @pl.when(ok)
        def _(i=i):
            r = req[i]
            w = jnp.minimum(starts[r] // 128, (4096 - WIN) // 128) * 128
            win = pl.ds(pl.multiple_of(w, 128), WIN)
            rr = pl.ds(pl.multiple_of(r * 64, 64), 64)
            q = qv[rr, :]
            x3 = selfs[rr, :][:, :1]
            x1 = dot_nn(q, kt[:, win])
            col = lax.broadcasted_iota(jnp.int32, (64, WIN), 1) + w
            x1 = jnp.where((col >= starts[r]) & (col < starts[r + 1]), x1, LOW)
            x2 = dot_nt(q, arr[...])
            slot = lax.broadcasted_iota(jnp.int32, (64, 128), 1) // 32
            seen = (slot == 0) & ((0 < n) & (req[0] == r))
            for j in range(1, 4):
                seen = seen | ((slot == j) & ((j < n) & (req[j] == r)))
            x2 = jnp.where(seen, x2, LOW)
            m = jnp.maximum(
                x3,
                jnp.maximum(jnp.max(x1, axis=1, keepdims=True), jnp.max(x2, axis=1, keepdims=True)),
            )
            e1 = jnp.exp2((x1 - m) * SCALE)
            e2 = jnp.exp2((x2 - m) * SCALE)
            e3 = jnp.exp2((x3 - m) * SCALE)
            l = jnp.sum(e1, axis=1, keepdims=True) + jnp.sum(e2, axis=1, keepdims=True) + e3
            o = dot_nt(e1.astype(BF16), kt[:LAT, win]) + dot_nn(e2.astype(BF16), arr[:, :LAT])
            o = o + e3 * latf[pl.ds(r, 1), :LAT]
            ob[i] = (o * (1.0 / l)).astype(BF16)

    for c in range(16):
        o_copy(c).wait()

    def fix_copy(i):
        return pltpu.make_async_copy(
            ob.at[i], out_hbm.at[pl.ds(pl.multiple_of(req[i] * 64, 64), 64), :], fsem.at[i]
        )

    for i in range(4):
        @pl.when(writes[i])
        def _(i=i):
            fix_copy(i).start()

    for i in range(4):
        @pl.when(writes[i])
        def _(i=i):
            fix_copy(i).wait()


def attend_kernel(
    q_hbm, kt_hbm, lat_hbm, len_hbm, owner_hbm, request_hbm, kv_hbm, blk_hbm, out_hbm,
    qv, kv, bias, ps0, ps1, pp0, pp1, pl0, pl1,
    kt, lat, latf, ov, selfs, s0, s1, p0, p1, m0, m1, l0, l1, mrun, lrun, acc, arr, ob,
    starts, pc, pt, req, src, len_ref, owner, request, qsem, ksem, lsem, asem, osem, fsem, isem,
):
    side = lax.axis_index("side")

    @pl.when(side == 0)
    def _():
        prefill_side(
            q_hbm, kv_hbm, out_hbm, qv, kv, ov, bias, ps0, ps1, pp0, pp1, pl0, pl1, qsem, ksem, osem
        )

    @pl.when(side == 1)
    def _():
        small = [
            pltpu.make_async_copy(a, b, isem.at[n])
            for n, (a, b) in enumerate(
                ((len_hbm, len_ref), (owner_hbm, owner), (request_hbm, request))
            )
        ]
        for c in small:
            c.start()
        for c in small:
            c.wait()
        decode_side(
            q_hbm, kt_hbm, lat_hbm, blk_hbm, len_ref, owner, request, out_hbm,
            qv, kt, lat, latf, ov, selfs, s0, s1, p0, p1, m0, m1, l0, l1, mrun, lrun, acc, arr, ob,
            starts, pc, pt, req, src, qsem, ksem, lsem, asem, osem, fsem,
        )


def attend(q, kt, latent, lengths, owner, request, kv, blocks):
    any_ = pl.BlockSpec(memory_space=pltpu.HBM)
    v = pltpu.VMEM
    i32 = jnp.int32
    dma = pltpu.SemaphoreType.DMA
    return pl.pallas_call(
        attend_kernel,
        out_shape=jax.ShapeDtypeStruct((VEC, LAT), BF16),
        in_specs=[any_] * 8,
        out_specs=any_,
        scratch_shapes=[
            v((VEC, WIDE), BF16), v((2048, WIDE), BF16), v((64, 1024), F32),
            v((BQ, 2048), F32), v((BQ, 2048), F32), v((BQ, 2048), BF16), v((BQ, 2048), BF16),
            v((BQ, 128), F32), v((BQ, 128), F32),
            v((WIDE, 4096), BF16), v((64, WIDE), BF16), v((64, WIDE), F32), v((VEC, LAT), BF16),
            v((VEC, 128), F32),
            v((256, UNIT), F32), v((256, UNIT), F32), v((256, UNIT), BF16), v((256, UNIT), BF16),
            v((256, 128), F32), v((256, 128), F32), v((256, 128), F32), v((256, 128), F32),
            v((256, 128), F32), v((256, 128), F32), v((256, LAT), F32),
            v((128, WIDE), BF16), v((4, 64, LAT), BF16),
            pltpu.SMEM((65,), i32), pltpu.SMEM((PAIRS,), i32), pltpu.SMEM((PAIRS,), i32),
            pltpu.SMEM((4,), i32), pltpu.SMEM((4,), i32),
            pltpu.SMEM((1, 64), i32), pltpu.SMEM((128,), i32), pltpu.SMEM((128,), i32),
            dma((16,)), dma((16,)), dma, dma((4,)), dma((16,)), dma((4,)), dma((3,)),
        ],
        compiler_params=pltpu.CompilerParams(vmem_limit_bytes=60 << 20),
        name="attend",
    )(q, kt, latent, lengths, owner, request, kv, blocks)


def local(queries, stream_rows, span_latents, decode_cache, cache_lengths, block_owner, block_request):
    q = queries.reshape(VEC, WIDE)
    stream = stream_rows.reshape(ROWS, WIDE)
    span = span_latents.reshape(ROWS, WIDE)
    owner = block_owner.reshape(128)
    kv, blocks = gather(stream, span, owner)
    out = attend(q, decode_cache.T, stream, cache_lengths, owner, block_request, kv, blocks)
    return out.reshape(1, 1, ROWS, HEADS, LAT)


def solution(mesh):
    return jax.shard_map(
        local,
        mesh=mesh,
        in_specs=(
            P("side", "grp", "seq", None, None),
            P("side", "grp", "seq", None),
            P("grp", "seq", None),
            P(("grp", "seq"), None),
            P(("grp", "seq"), None),
            P(),
            P(),
        ),
        out_specs=P("side", "grp", "seq", None, None),
        check_vma=False,
    )
```
